256 devices in a mesh: lat: 4 (over y_lo, core), lon: 64 (over y_hi, x, z).
Axes of the slice: x: 4, y: 4 (y_hi: 2, y_lo: 2; y = y_hi * 2 + y_lo), z: 8, core: 2. Of those that a mesh axis runs over, the one named last changes fastest.
Arguments:
- resid: bfloat16 [28, 1344, 1024], P('lat', 'lon'), may hold values from -8 to 8
- qkv: bfloat16 [28, 1344, 3, 1024], P('lat', 'lon'), may hold values from -40 to 40
- out_proj: bfloat16 [1024, 1024], replicated, may hold values from -0.1875 to 0.1875
- norm_gain: float32 [1024], replicated, may hold values from 0.5 to 1.5
- router: float32 [1024, 64], replicated, may hold values from -2 to 2
- w_in: bfloat16 [64, 1024, 4096], P('lon', None, 'lat'), may hold values from -0.1875 to 0.1875
- w_out: bfloat16 [64, 4096, 1024], P('lon', 'lat'), may hold values from -0.09375 to 0.09375
- expert_ids: int32 [28, 1344, 2], P('lat', 'lon'), may hold values from 0 to 63, as said below
- slots: int32 [28, 1344, 2], P('lat', 'lon'), may hold values from 0 to 4, as said below
- shifts: int32 [4], replicated, may hold values from 0 to 6, as said below
- grad_out: bfloat16 [28, 1344, 1024], P('lat', 'lon'), may hold values from -6 to 6
Outputs:
- d_resid: bfloat16 [28, 1344, 1024], P('lat', 'lon')
- d_qkv: bfloat16 [28, 1344, 3, 1024], P('lat', 'lon')
- d_out_proj: float32 [1024, 1024], P(('lat', 'lon'))
- d_gain: float32 [1024], P(('lat', 'lon'))
- d_router: float32 [1024, 64], P(('lat', 'lon'))
- d_w_in: bfloat16 [64, 1024, 4096], P('lon', None, 'lat')
- d_w_out: bfloat16 [64, 4096, 1024], P('lon', 'lat')
The draws below stay inside these ranges and needn't reach their ends.
Inputs may be any that keep to these rules, and one draw needn't show every extreme that they name: `expert_ids`: within the patches of one device (7 rows by 21 columns) the two ids of a patch differ and no expert is named more than 5 times; in every draw one expert is named exactly 5 times in every device's patches. `slots`: within the patches of one device, the pairs (expert, slot) of all assignments are different. `shifts`: one band has the shift 6.
All inputs are finite; a program needn't handle non-finite values.
Results may differ from the reference program's by a relative error of at most 0.023.
Values may be sent and summed in bfloat16 or wider, within the bound.
No kernel may reach another device: no remote copies, remote signals or barrier semaphores. Data moves between devices by JAX's collectives and lax.ppermute only.
A program may use at most 128 MiB of HBM per device.

```python
import math
import jax
import jax.numpy as jnp
from jax import lax

D = 1024
NH = 32
FF = 4096
WIN = 7
COLS_DEV = 21
EXPERTS = 64
CAP = 5
ROWS = 28
COLS = 1344
N_LAT = 4
N_LON = 64


def draw_resid(key, part):
    row_scale = jnp.exp(jax.random.uniform(jax.random.fold_in(key, 5), (ROWS, COLS, 1), jnp.float32, math.log(0.05), math.log(0.5)))
    noise = jnp.clip(jax.random.normal(jax.random.fold_in(key, 1), (ROWS, COLS, D), jnp.float32), -6.0, 6.0)
    base = noise * row_scale
    return base.astype(jnp.bfloat16)


def draw_router(key, part):
    base = jnp.clip(jax.random.normal(jax.random.fold_in(key, 2), (D, EXPERTS), jnp.float32), -6.0, 6.0) * (0.3 / math.sqrt(D))
    return base


def draw_qkv(key, part):
    base = jnp.clip(jax.random.normal(jax.random.fold_in(key, 3), (ROWS, COLS, 3, D), jnp.float32), -6.0, 6.0)
    return base.astype(jnp.bfloat16)


def routing_table(key):
    tokens_here = WIN * COLS_DEV
    hot = jax.random.randint(jax.random.fold_in(key, 13), (), 0, EXPERTS)
    block_keys = jax.random.split(jax.random.fold_in(key, 11), N_LAT * N_LON)

    def one_block(block_key):
        key_one, key_two, key_three = jax.random.split(block_key, 3)
        order = jax.random.permutation(key_one, tokens_here)
        placed = jnp.argsort(order)
        others = jnp.sort(jax.random.permutation(key_two, (EXPERTS - 1) * CAP)[:2 * tokens_here - CAP]) + CAP
        spots = jnp.concatenate([jnp.arange(CAP), others])
        shuffled = jax.random.permutation(key_three, EXPERTS)
        where_hot = jnp.argsort(shuffled)[hot]
        labels = shuffled.at[where_hot].set(shuffled[0]).at[0].set(hot)
        first_spot = spots[placed]
        second_spot = spots[placed + tokens_here]
        picked = jnp.stack([labels[first_spot // CAP], labels[second_spot // CAP]], axis=-1)
        within = jnp.stack([first_spot % CAP, second_spot % CAP], axis=-1)
        return (picked, within)
    picked, within = jax.vmap(one_block)(block_keys)

    def to_grid(values):
        shaped = values.reshape(N_LAT, N_LON, WIN, COLS_DEV, 2)
        return shaped.transpose(0, 2, 1, 3, 4).reshape(ROWS, COLS, 2).astype(jnp.int32)
    return (to_grid(picked), to_grid(within))


def draw_expert_ids(key, part):
    return routing_table(key)[0]


def draw_slots(key, part):
    return routing_table(key)[1]


def draw_shifts(key, part):
    base = jax.random.randint(jax.random.fold_in(key, 21), (N_LAT,), 0, WIN)
    widest = jax.random.randint(jax.random.fold_in(key, 22), (), 0, N_LAT)
    return base.at[widest].set(WIN - 1).astype(jnp.int32)


def block_levels(stream_key, dims, pieces, smallest, high):
    gain, own = 1.0, jax.random.fold_in(stream_key, 6)
    for dim, parts in pieces:
        steps = jnp.exp(jax.random.uniform(jax.random.fold_in(own, dim), (parts,), jnp.float32, smallest / len(pieces), high / len(pieces)))
        gain = gain * jnp.repeat(steps, dims[dim] // parts).reshape([-1 if axis == dim else 1 for axis in range(len(dims))])
    return gain


def gaussian(stream_key, extent, deviation, most, pieces=(), kind=jnp.bfloat16):
    factor_of = block_levels(stream_key, extent, pieces, -0.22, 0.18) if pieces else 1.0
    result = jax.random.normal(stream_key, extent, jnp.float32) * deviation * factor_of
    return jnp.minimum(jnp.maximum(result, -most), most).astype(kind)


def setup_inputs(seed: int = 0) -> dict:
    arg_keys = jax.random.split(jax.random.key(seed), 12)
    resid = draw_resid(jax.random.fold_in(arg_keys[11], 71), 0)
    qkv = draw_qkv(jax.random.fold_in(arg_keys[11], 71), 0)
    out_proj = gaussian(arg_keys[2], (D, D), D ** -0.5, 0.1875)
    norm_gain = jnp.clip(1.0 + 0.1 * jax.random.normal(arg_keys[3], (D,), jnp.float32), 0.5, 1.5)
    router = draw_router(jax.random.fold_in(arg_keys[11], 71), 0)
    w_in = gaussian(arg_keys[5], (EXPERTS, D, FF), D ** -0.5, 0.1875, ((0, 64), (2, 4)))
    w_out = gaussian(arg_keys[6], (EXPERTS, FF, D), FF ** -0.5, 0.09375, ((0, 64), (1, 4)))
    expert_ids = draw_expert_ids(jax.random.fold_in(arg_keys[11], 71), 0)
    slots = draw_slots(jax.random.fold_in(arg_keys[11], 71), 0)
    shifts = draw_shifts(jax.random.fold_in(arg_keys[11], 71), 0)
    grad_out = gaussian(arg_keys[10], (ROWS, COLS, D), 1.0, 6.0, ((0, 4), (1, 64)))
    return {"resid": resid, "qkv": qkv, "out_proj": out_proj, "norm_gain": norm_gain, "router": router, "w_in": w_in, "w_out": w_out, "expert_ids": expert_ids, "slots": slots, "shifts": shifts, "grad_out": grad_out}


norm_eps = 1e-05
zloss_weight = 0.25
highest = lax.Precision.HIGHEST

def gelu_pair(hidden):
    normal_cdf = 0.5 * (1.0 + lax.erf(hidden * 0.7071067811865476))
    return (hidden * normal_cdf, normal_cdf + hidden * jnp.exp(-0.5 * hidden * hidden) * 0.3989422804014327)

def to_windows(values):
    height, breadth = (values.shape[0], values.shape[1])
    shaped = values.reshape(height, breadth // WIN, WIN, NH, D // NH)
    return shaped.transpose(1, 3, 0, 2, 4).reshape(breadth // WIN, NH, height * WIN, D // NH)

def from_windows(blocks, height):
    number = blocks.shape[0]
    shaped = blocks.reshape(number, NH, height, WIN, D // NH)
    return shaped.transpose(2, 0, 3, 1, 4).reshape(height, number * WIN, D)

def attend_forward(queries, keyset, values):
    factor = queries.shape[-1] ** (-0.5)
    scores = jnp.einsum('wnqd,wnkd->wnqk', queries.astype(jnp.float32), keyset.astype(jnp.float32), precision=highest) * factor
    row_max = lax.optimization_barrier(jnp.max(scores, axis=-1, keepdims=True))
    raised = jnp.exp(scores - row_max)
    weights_hi = raised / lax.optimization_barrier(jnp.sum(raised, axis=-1, keepdims=True))
    weights_lo = weights_hi.astype(jnp.bfloat16)
    attended = jnp.einsum('wnqk,wnkd->wnqd', weights_lo.astype(jnp.float32), values.astype(jnp.float32), precision=highest).astype(jnp.bfloat16)
    return (weights_hi, weights_lo, attended)

def attend_backward(queries, keyset, values, weights_hi, weights_lo, upstream):
    factor = queries.shape[-1] ** (-0.5)
    up_wide = upstream.astype(jnp.float32)
    grad_weights = jnp.einsum('wnqd,wnkd->wnqk', up_wide, values.astype(jnp.float32), precision=highest)
    grad_scores = (weights_hi * (grad_weights - lax.optimization_barrier(jnp.sum(grad_weights * weights_hi, axis=-1, keepdims=True))) * factor).astype(jnp.bfloat16)
    score_wide = grad_scores.astype(jnp.float32)
    grad_queries = jnp.einsum('wnqk,wnkd->wnqd', score_wide, keyset.astype(jnp.float32), precision=highest).astype(jnp.bfloat16)
    grad_keys = jnp.einsum('wnqk,wnqd->wnkd', score_wide, queries.astype(jnp.float32), precision=highest).astype(jnp.bfloat16)
    grad_values = jnp.einsum('wnqk,wnqd->wnkd', weights_lo.astype(jnp.float32), up_wide, precision=highest).astype(jnp.bfloat16)
    return (grad_queries, grad_keys, grad_values)

def roll_columns(values, shifted):
    breadth = values.shape[1]
    doubled = jnp.concatenate([values, values], axis=1)
    return lax.dynamic_slice_in_dim(doubled, breadth - shifted, breadth, 1)

def unroll_columns(values, shifted):
    breadth = values.shape[1]
    doubled = jnp.concatenate([values, values], axis=1)
    return lax.dynamic_slice_in_dim(doubled, shifted, breadth, 1)

def expert_step(operands):
    slot_in, slot_grad, slot_comb, weight_in, weight_out = operands
    in_wide = slot_in.astype(jnp.float32)
    grad_wide = slot_grad.astype(jnp.float32)
    hidden = jnp.dot(in_wide, weight_in.astype(jnp.float32), precision=highest)
    activated, gelu_slope = gelu_pair(hidden)
    grad_w = jnp.dot(grad_wide, weight_out.astype(jnp.float32).T, precision=highest)
    comb_low = lax.optimization_barrier(jnp.sum(activated * grad_w, axis=-1)).astype(jnp.bfloat16)
    comb_wide = slot_comb.astype(jnp.float32)[:, None]
    scaled_act = (comb_wide * activated).astype(jnp.bfloat16)
    grad_out_w = jnp.dot(scaled_act.astype(jnp.float32).T, grad_wide, precision=highest).astype(jnp.bfloat16)
    grad_hidden = (comb_wide * grad_w * gelu_slope).astype(jnp.bfloat16)
    hidden_wide = grad_hidden.astype(jnp.float32)
    grad_in_w = jnp.dot(in_wide.T, hidden_wide, precision=highest).astype(jnp.bfloat16)
    slot_low = jnp.dot(hidden_wide, weight_in.astype(jnp.float32).T, precision=highest).astype(jnp.bfloat16)
    return (grad_in_w, grad_out_w, slot_low, comb_low)

def reference(resid, qkv, out_proj, norm_gain, router, w_in, w_out, expert_ids, slots, shifts, grad_out):
    height, breadth, features = resid.shape
    tokens_all = height * breadth
    experts_all = router.shape[1]
    per_expert = N_LAT * N_LON * CAP
    resid_wide = resid.reshape(tokens_all, features).astype(jnp.float32)
    center = resid_wide - lax.optimization_barrier(jnp.mean(resid_wide, axis=-1, keepdims=True))
    inv_std = lax.rsqrt(lax.optimization_barrier(jnp.mean(center * center, axis=-1, keepdims=True)) + norm_eps)
    normed = center * inv_std
    routed_in = (normed * norm_gain).astype(jnp.bfloat16)
    logits = jnp.dot(routed_in.astype(jnp.float32), router, precision=highest)
    row_max = lax.optimization_barrier(jnp.max(logits, axis=-1, keepdims=True))
    shifted_exp = jnp.exp(logits - row_max)
    totals = lax.optimization_barrier(jnp.sum(shifted_exp, axis=-1, keepdims=True))
    router_probs = shifted_exp / totals
    log_total = row_max + jnp.log(totals)
    picked_ids = expert_ids.reshape(tokens_all, 2)
    picked_slots = slots.reshape(tokens_all, 2)
    one_hot = (picked_ids[:, :, None] == jnp.arange(experts_all, dtype=jnp.int32)[None, None, :]).astype(jnp.float32)
    combine = lax.optimization_barrier(jnp.sum(one_hot * router_probs[:, None, :], axis=-1)).astype(jnp.bfloat16)
    lat_block = (jnp.arange(height, dtype=jnp.int32) // WIN)[:, None]
    lon_block = (jnp.arange(breadth, dtype=jnp.int32) // COLS_DEV)[None, :]
    source = (lat_block * N_LON + lon_block).reshape(tokens_all, 1).astype(jnp.int32)
    targets = (picked_ids * per_expert + source * CAP + picked_slots).astype(jnp.int32)
    flat_targets = targets.reshape(-1)
    grad_rows = grad_out.reshape(tokens_all, features)
    total_slots = experts_all * per_expert
    buffer_in = jnp.zeros((total_slots, features), jnp.bfloat16).at[flat_targets].set(jnp.repeat(routed_in, 2, axis=0))
    buffer_grad = jnp.zeros((total_slots, features), jnp.bfloat16).at[flat_targets].set(jnp.repeat(grad_rows, 2, axis=0))
    buffer_comb = jnp.zeros((total_slots,), jnp.bfloat16).at[flat_targets].set(combine.reshape(-1))
    grad_in_w, grad_out_w, slot_grads, comb_grads = lax.map(expert_step, (buffer_in.reshape(experts_all, per_expert, features), buffer_grad.reshape(experts_all, per_expert, features), buffer_comb.reshape(experts_all, per_expert), w_in, w_out))
    slot_grads = lax.optimization_barrier(slot_grads)
    comb_grads = lax.optimization_barrier(comb_grads)
    routed_grad = slot_grads.reshape(total_slots, features)[flat_targets].reshape(tokens_all, 2, features).astype(jnp.float32)
    assign_grad = comb_grads.reshape(total_slots)[flat_targets].reshape(tokens_all, 2).astype(jnp.float32)
    grad_probs = lax.optimization_barrier(jnp.sum(one_hot * assign_grad[:, :, None], axis=1))
    grad_logits = router_probs * (grad_probs - lax.optimization_barrier(jnp.sum(router_probs * grad_probs, axis=-1, keepdims=True))) + 2.0 * zloss_weight * log_total * router_probs
    grad_normed_out = routed_grad[:, 0] + routed_grad[:, 1] + jnp.dot(grad_logits, router.T, precision=highest)
    d_gain = lax.optimization_barrier(jnp.sum(grad_normed_out * normed, axis=0))
    grad_normed = grad_normed_out * norm_gain
    grad_resid = grad_rows.astype(jnp.float32) + inv_std * (grad_normed - lax.optimization_barrier(jnp.mean(grad_normed, axis=-1, keepdims=True)) - normed * lax.optimization_barrier(jnp.mean(grad_normed * normed, axis=-1, keepdims=True)))
    d_resid = grad_resid.astype(jnp.bfloat16)
    d_router = jnp.dot(routed_in.astype(jnp.float32).T, grad_logits, precision=highest)
    d_attn = jnp.dot(d_resid.astype(jnp.float32), out_proj.astype(jnp.float32).T, precision=highest).astype(jnp.bfloat16).reshape(height, breadth, features)
    attended_rows = []
    grad_bands = []
    for band_index in range(N_LAT):
        shifted = shifts[band_index]
        first_row = band_index * WIN
        rolled = roll_columns(qkv[first_row:first_row + WIN], shifted)
        rolled_grad = roll_columns(d_attn[first_row:first_row + WIN], shifted)
        queries = to_windows(rolled[:, :, 0])
        keyset = to_windows(rolled[:, :, 1])
        values = to_windows(rolled[:, :, 2])
        weights_hi, weights_lo, attended = attend_forward(queries, keyset, values)
        grad_queries, grad_keys, grad_values = attend_backward(queries, keyset, values, weights_hi, weights_lo, to_windows(rolled_grad))
        attended_rows.append(unroll_columns(from_windows(attended, WIN), shifted))
        stacked = jnp.stack([from_windows(grad_queries, WIN), from_windows(grad_keys, WIN), from_windows(grad_values, WIN)], axis=2)
        grad_bands.append(unroll_columns(stacked, shifted))
    attended_all = jnp.concatenate(attended_rows, axis=0).reshape(tokens_all, features)
    d_qkv = jnp.concatenate(grad_bands, axis=0)
    d_out_proj = jnp.dot(attended_all.astype(jnp.float32).T, d_resid.astype(jnp.float32), precision=highest)
    return (d_resid.reshape(height, breadth, features), d_qkv, d_out_proj, d_gain, d_router, grad_in_w, grad_out_w)
```

```python
import functools

import jax
import jax.numpy as jnp
from jax import lax
from jax.experimental import pallas as pl
from jax.experimental.pallas import tpu as pltpu
from jax.sharding import PartitionSpec as P

D = 1024
NH = 32
WIN = 7
ROWS_DEV = 7
COLS_DEV = 21
PITCH = 24
TOK = ROWS_DEV * PITCH
EXPERTS = 64
CAP = 5
LANES = 128
BLOCKS = D // LANES
SLOTS = EXPERTS * CAP
SEND_ROWS = 2 * CAP * BLOCKS
BACK_ROWS = CAP * BLOCKS + 8
SHARE_ROWS = 40
PAY_ROWS = TOK + 8
WIDE = D + LANES

norm_eps = 1e-05
zloss_weight = 0.25
bf16 = jnp.bfloat16
f32 = jnp.float32
MEBI = 1024 * 1024


def call(kernel, vmem, out_shape, flops, moved, scratch=(), **kwargs):
    return pl.pallas_call(
        kernel,
        out_shape=out_shape,
        scratch_shapes=list(scratch),
        compiler_params=pltpu.CompilerParams(vmem_limit_bytes=vmem * MEBI),
        cost_estimate=pl.CostEstimate(flops=flops, bytes_accessed=moved, transcendentals=0),
        **kwargs,
    )


def mm(left, right):
    return lax.dot_general(left, right, (((1,), (0,)), ((), ())), preferred_element_type=f32)


def mm_cols(left, right):
    return lax.dot_general(left, right, (((1,), (1,)), ((), ())), preferred_element_type=f32)


def mm_rows(left, right):
    return lax.dot_general(left, right, (((0,), (0,)), ((), ())), preferred_element_type=f32)


def shape(dims, kind):
    return jax.ShapeDtypeStruct(dims, kind)


def iota(dims, axis):
    return lax.broadcasted_iota(jnp.int32, dims, axis)


def split3(value):
    high = value.astype(bf16)
    rest = value - high.astype(f32)
    middle = rest.astype(bf16)
    return (high, middle, (rest - middle.astype(f32)).astype(bf16))


def softmax_parts(logits):
    held = jnp.where(iota(logits.shape, 1) < EXPERTS, logits, -1e30)
    top = jnp.max(held, axis=-1, keepdims=True)
    raised = jnp.exp(held - top)
    total = jnp.sum(raised, axis=-1, keepdims=True)
    return (raised / total, top + jnp.log(total))


def three_logits(rows, split_router):
    triple = mm_cols(rows, split_router)
    return triple[:, 2 * LANES :] + triple[:, LANES : 2 * LANES] + triple[:, :LANES]


def front_kernel(
    resid_ref, grad_ref, gain_ref, router_ref, ids_ref, slots_ref,
    send_ref, split_ref, z_ref, normed_ref, stats_ref, back_ref, rows, folded, target_ref,
):
    target_ref[...] = jnp.full((2, 2 * TOK), -1, jnp.int32)
    back_ref[...] = jnp.full((2, TOK), -1, jnp.int32)
    for row in range(ROWS_DEV):
        ids = ids_ref[row]
        spots = slots_ref[row]
        base = row * PITCH
        back_ref[:, base : base + COLS_DEV] = spots * EXPERTS + ids
        target_ref[:, base : base + COLS_DEV] = ids * (2 * CAP) + spots
        target_ref[:, TOK + base : TOK + base + COLS_DEV] = ids * (2 * CAP) + spots + CAP
    rows[...] = jnp.zeros_like(rows)
    for row in range(ROWS_DEV):
        rows[row * PITCH : row * PITCH + COLS_DEV, :] = resid_ref[row].astype(f32)
        base = TOK + row * PITCH
        rows[base : base + COLS_DEV, :] = grad_ref[row].astype(f32)
    resid = rows[:TOK, :]
    center = resid - jnp.mean(resid, axis=-1, keepdims=True)
    inv_std = lax.rsqrt(jnp.mean(center * center, axis=-1, keepdims=True) + norm_eps)
    normed = center * inv_std
    normed_ref[...] = normed
    rows[:TOK, :] = normed * gain_ref[...]
    both = rows[...].astype(bf16)
    slot = iota((2 * SLOTS, 2 * TOK), 0)
    pick = jnp.where(
        (slot == target_ref[0:1, :]) | (slot == target_ref[1:2, :]), 1.0, 0.0
    ).astype(bf16)
    for pair in range(BLOCKS // 2):
        got = mm(pick, both[:, pair * 2 * LANES : (pair + 1) * 2 * LANES])
        for half in range(2):
            folded[pl.ds(2 * pair + half, 2 * SLOTS, stride=BLOCKS), :] = got[
                :, half * LANES : (half + 1) * LANES
            ]
    send_ref[...] = folded[...].astype(bf16)
    empty = jnp.zeros((LANES - EXPERTS, D), bf16)
    for index, part in enumerate(split3(router_ref[...])):
        split_ref[index * LANES : index * LANES + EXPERTS, :] = part
        split_ref[index * LANES + EXPERTS : (index + 1) * LANES, :] = empty
    z_ref[...] = jnp.where(iota((PAY_ROWS, 1), 0) < TOK, rows[:PAY_ROWS, :], 0.0).astype(bf16)
    probs, log_total = softmax_parts(three_logits(both[:PAY_ROWS, :], split_ref[...]))
    stats_ref[:, :LANES] = probs[:TOK]
    stats_ref[:, LANES : 2 * LANES] = jnp.broadcast_to(log_total[:TOK], (TOK, LANES))
    stats_ref[:, 2 * LANES :] = jnp.broadcast_to(inv_std, (TOK, LANES))


def front(resid, grad, gain, router_t, ids, slots):
    return call(
        front_kernel,
        56,
        (
            shape((EXPERTS * SEND_ROWS, LANES), bf16),
            shape((3 * LANES, D), bf16),
            shape((PAY_ROWS, D), bf16),
            shape((TOK, D), f32),
            shape((TOK, 3 * LANES), f32),
            shape((2, TOK), jnp.int32),
        ),
        4_600_000_000,
        4_000_000,
        [
            pltpu.VMEM((2 * TOK, D), f32),
            pltpu.VMEM((EXPERTS * SEND_ROWS, LANES), f32),
            pltpu.VMEM((2, 2 * TOK), jnp.int32),
        ],
    )(resid, grad, gain, router_t, ids, slots)


PARTS = (3 * EXPERTS, 2 * EXPERTS)


def unfold_kernel(got_ref, first_ref, second_ref, wide):
    wide[...] = got_ref[...].astype(f32)
    for c in range(2 * CAP):
        ref, place = (first_ref, c % CAP) if c % CAP < 3 else (second_ref, c % CAP - 3)
        base = place * EXPERTS + (c // CAP) * ref.shape[0] // 2
        for s in range(BLOCKS):
            ref[base : base + EXPERTS, s * LANES : (s + 1) * LANES] = wide[
                pl.ds(c * BLOCKS + s, EXPERTS, stride=SEND_ROWS), :
            ].astype(bf16)


def unfold(got):
    return call(
        unfold_kernel,
        14,
        tuple(shape((2 * part, D), bf16) for part in PARTS),
        3_900_000_000,
        2_600_000,
        [pltpu.VMEM((EXPERTS * SEND_ROWS, LANES), f32)],
    )(got)


FF_TILE = 256


def expert_kernel(count, expert_ref, *refs):
    chunks = refs[:count]
    in_ref, out_w_ref, split_ref, near_ref, far_ref, cu_ref, dh_ref = refs[count : count + 7]
    inputs, grads, total, dc, comb = refs[count + 7 :]
    step = pl.program_id(0)
    rows = inputs.shape[0]

    @pl.when(step == 0)
    def _():
        base = 0
        for ref in chunks:
            part = ref.shape[0] // 2
            inputs[base : base + part, :] = ref[:part, :]
            grads[base : base + part, :] = ref[part:, :]
            base += part
        probs, _unused = softmax_parts(three_logits(inputs[...], split_ref[...]))
        mine = jnp.where(iota(probs.shape, 1) == expert_ref[0], probs, 0.0)
        weight = jnp.sum(mine, axis=-1, keepdims=True).astype(bf16).astype(f32)
        comb[...] = jnp.broadcast_to(weight, (rows, LANES))
        dc[...] = jnp.zeros_like(dc)
        total[...] = jnp.zeros_like(total)

    weight_in = in_ref[...]
    hidden = mm(inputs[...], weight_in)
    grad_w = mm_cols(grads[...], out_w_ref[...])
    cdf = 0.5 * (1.0 + lax.erf(hidden * 0.7071067811865476))
    active = hidden * cdf
    slope = cdf + hidden * jnp.exp(-0.5 * hidden * hidden) * 0.3989422804014327
    dc[...] += jnp.broadcast_to(jnp.sum(active * grad_w, axis=-1, keepdims=True), (rows, LANES))
    weight = comb[:, 0:1]
    cu_ref[...] = (weight * active).astype(bf16)
    grad_hidden = (weight * grad_w * slope).astype(bf16)
    dh_ref[...] = grad_hidden
    total[...] += mm_cols(grad_hidden, weight_in)

    @pl.when(step == pl.num_programs(0) - 1)
    def _():
        for index, ref in enumerate((near_ref, far_ref)):
            span = slice(index * rows // 2, (index + 1) * rows // 2)
            ref[:, :D] = total[span, :].astype(bf16)
            ref[:, D:] = dc[span, :].astype(bf16)


def experts(expert, chunks, weight_in, weight_out, split_router):
    width = weight_in.shape[1]
    count = len(chunks)
    rows = sum(chunk.shape[0] for chunk in chunks) // 2
    whole = lambda dims: pl.BlockSpec(dims, lambda j: (0,) * len(dims))
    return call(
        functools.partial(expert_kernel, count),
        56 if count == 4 else 30,
        (
            shape((rows // 2, WIDE), bf16),
            shape((rows // 2, WIDE), bf16),
            shape((rows, width), bf16),
            shape((rows, width), bf16),
        ),
        22 * rows * D * width,
        12_000_000,
        [
            pltpu.VMEM((rows, D), bf16),
            pltpu.VMEM((rows, D), bf16),
            pltpu.VMEM((rows, D), f32),
            pltpu.VMEM((rows, LANES), f32),
            pltpu.VMEM((rows, LANES), f32),
        ],
        grid=(width // FF_TILE,),
        in_specs=[pl.BlockSpec(memory_space=pltpu.SMEM)]
        + [whole(chunk.shape) for chunk in chunks]
        + [
            pl.BlockSpec((D, FF_TILE), lambda j: (0, j)),
            pl.BlockSpec((FF_TILE, D), lambda j: (j, 0)),
            whole((3 * LANES, D)),
        ],
        out_specs=(
            whole((rows // 2, WIDE)),
            whole((rows // 2, WIDE)),
            pl.BlockSpec((rows, FF_TILE), lambda j: (0, j)),
            pl.BlockSpec((rows, FF_TILE), lambda j: (0, j)),
        ),
    )(expert, *chunks, weight_in, weight_out, split_router)


def fold_kernel(own_ref, near_ref, first_ref, second_ref, out_ref, folded, total):
    total[...] = own_ref[...].astype(f32) + near_ref[...].astype(f32)
    total[: PARTS[0], :] += first_ref[...].astype(f32)
    total[PARTS[0] :, :] += second_ref[...].astype(f32)
    for c in range(CAP):
        part = total[c * EXPERTS : (c + 1) * EXPERTS, :]
        for s in range(BLOCKS):
            folded[pl.ds(c * BLOCKS + s, EXPERTS, stride=BACK_ROWS), :] = part[
                :, s * LANES : (s + 1) * LANES
            ]
        folded[pl.ds(CAP * BLOCKS + c, EXPERTS, stride=BACK_ROWS), :] = part[:, D:]
    for spare in range(CAP * BLOCKS + CAP, BACK_ROWS):
        folded[pl.ds(spare, EXPERTS, stride=BACK_ROWS), :] = jnp.zeros((EXPERTS, LANES), f32)
    out_ref[...] = folded[...].astype(bf16)


def fold(own, near, first, second):
    return call(
        fold_kernel,
        14,
        shape((EXPERTS * BACK_ROWS, LANES), bf16),
        3_800_000_000,
        3_000_000,
        [pltpu.VMEM((EXPERTS * BACK_ROWS, LANES), f32), pltpu.VMEM((SLOTS, WIDE), f32)],
    )(own, near, first, second)


def middle_kernel(
    back_ref, target_ref, normed_ref, stats_ref, grad_ref, gain_ref, router_ref, proj_ref,
    resid_ref, attn_ref, pay_ref, wide, table, rows,
):
    wide[...] = back_ref[...].astype(f32)
    lane = iota((EXPERTS, LANES), 1)
    same = lane == iota((EXPERTS, LANES), 0)
    for c in range(CAP):
        span = slice(c * EXPERTS, (c + 1) * EXPERTS)
        for s in range(BLOCKS):
            table[span, s * LANES : (s + 1) * LANES] = wide[
                pl.ds(c * BLOCKS + s, EXPERTS, stride=BACK_ROWS), :
            ].astype(bf16)
        weights = wide[pl.ds(CAP * BLOCKS + c, EXPERTS, stride=BACK_ROWS), :]
        table[span, D:] = jnp.where(same, weights, 0.0).astype(bf16)
    slot = iota((SLOTS, TOK), 0)
    pick = jnp.where(
        (slot == target_ref[0:1, :]) | (slot == target_ref[1:2, :]), 1.0, 0.0
    ).astype(bf16)
    routed = mm_rows(pick, table[...])
    grad_probs = routed[:, D:]
    probs = stats_ref[:, :LANES]
    log_total = stats_ref[:, LANES : 2 * LANES]
    inv_std = stats_ref[:, 2 * LANES : 2 * LANES + 1]
    grad_logits = (
        probs * (grad_probs - jnp.sum(probs * grad_probs, axis=-1, keepdims=True))
        + 2.0 * zloss_weight * log_total * probs
    )
    grad_z = routed[:, :D] + jnp.dot(
        grad_logits[:, :EXPERTS], router_ref[...], precision=lax.Precision.HIGHEST,
        preferred_element_type=f32,
    )
    normed = normed_ref[...]
    gain_term = jnp.sum(grad_z * normed, axis=0, keepdims=True)
    rows[...] = jnp.zeros_like(rows)
    for row in range(ROWS_DEV):
        rows[row * PITCH : row * PITCH + COLS_DEV, :] = grad_ref[row].astype(f32)
    grad_normed = grad_z * gain_ref[...]
    rows[:TOK, :] = rows[:TOK, :] + inv_std * (
        grad_normed
        - jnp.mean(grad_normed, axis=-1, keepdims=True)
        - normed * jnp.mean(grad_normed * normed, axis=-1, keepdims=True)
    )
    for row in range(ROWS_DEV):
        resid_ref[row] = rows[row * PITCH : row * PITCH + COLS_DEV, :].astype(bf16)
    low = rows[...].astype(bf16)
    rows[...] = mm_cols(low, proj_ref[...])
    for row in range(ROWS_DEV):
        attn_ref[row] = rows[row * PITCH : row * PITCH + COLS_DEV, :].astype(bf16)
    high, middle, last = (part.astype(f32) for part in split3(gain_term))
    extra = iota((PAY_ROWS, 1), 0)
    rows[...] = jnp.where(
        extra < TOK,
        low.astype(f32),
        jnp.where(
            extra == TOK, high, jnp.where(extra == TOK + 1, middle, jnp.where(extra == TOK + 2, last, 0.0))
        ),
    )
    pay_ref[:, :D] = rows[...].astype(bf16)
    upper = grad_logits.astype(bf16).astype(f32)
    lower = (grad_logits - upper).astype(bf16).astype(f32)
    mixed = upper + pltpu.roll(lower, EXPERTS, 1)
    pay_ref[:, D:] = jnp.concatenate([mixed, jnp.zeros((PAY_ROWS - TOK, LANES), f32)], axis=0).astype(bf16)


def middle(back, targets, normed, stats, grad, gain, router_t, out_proj):
    return call(
        middle_kernel,
        56,
        (
            shape((ROWS_DEV, COLS_DEV, D), bf16),
            shape((ROWS_DEV, COLS_DEV, D), bf16),
            shape((PAY_ROWS, WIDE), bf16),
        ),
        7_000_000_000,
        6_000_000,
        [
            pltpu.VMEM((EXPERTS * BACK_ROWS, LANES), f32),
            pltpu.VMEM((SLOTS, WIDE), bf16),
            pltpu.VMEM((PAY_ROWS, D), f32),
        ],
    )(back, targets, normed, stats, grad, gain, router_t, out_proj)


SHARED = EXPERTS * SHARE_ROWS
QUARTER = D // 4


def share_kernel(core_ref, pay_ref, pay_near_ref, side_ref, side_near_ref, out_ref, folded):
    both = ((pay_ref, side_ref), (pay_near_ref, side_near_ref))
    gain = jnp.zeros((1, D), f32)
    at = iota((16, 1), 0)
    for pay, _unused in both:
        last = pay[PAY_ROWS - 16 :, :D].astype(f32)
        gain += jnp.sum(jnp.where((at >= 8) & (at < 11), last, 0.0), axis=0, keepdims=True)
    same = iota((QUARTER, QUARTER), 0) == iota((QUARTER, QUARTER), 1)
    lane = iota((QUARTER, LANES), 1)
    step = SHARE_ROWS // 4
    for block in range(2):
        z_at = slice(block * QUARTER, (block + 1) * QUARTER)
        a_at = slice((2 + block) * QUARTER, (3 + block) * QUARTER)
        proj = sum(mm_rows(side[:, a_at], pay[:, :D]) for pay, side in both)
        router = sum(mm_rows(side[:, z_at], pay[:, D:]) for pay, side in both)
        mine = jnp.zeros((1, QUARTER), f32)
        for core in range(2):
            place = (2 * block + core) * QUARTER
            mine += jnp.where(core_ref[0] == core, gain[:, place : place + QUARTER], 0.0)
        column = jnp.sum(jnp.where(same, mine, 0.0), axis=-1, keepdims=True)
        router = router + pltpu.roll(router, EXPERTS, 1)
        extra = jnp.where(lane < EXPERTS, router, jnp.where(lane == EXPERTS, column, 0.0))
        upper = extra.astype(bf16).astype(f32)
        base = block * SHARED
        for s in range(BLOCKS):
            folded[pl.ds(base + s, QUARTER, stride=step), :] = proj[:, s * LANES : (s + 1) * LANES]
        folded[pl.ds(base + BLOCKS, QUARTER, stride=step), :] = upper
        folded[pl.ds(base + BLOCKS + 1, QUARTER, stride=step), :] = extra - upper
    out_ref[...] = folded[...].astype(bf16)


def share(core, *arrays):
    inner = pl.BlockSpec(memory_space=pltpu.VMEM)
    return call(
        share_kernel,
        20,
        shape((2 * SHARED, LANES), bf16),
        3_900_000_000,
        4_000_000,
        [pltpu.VMEM((2 * SHARED, LANES), f32)],
        in_specs=[pl.BlockSpec(memory_space=pltpu.SMEM)] + [inner] * 4,
    )(core, *arrays)


def tally_kernel(got_ref, out_ref):
    out_ref[...] = sum(got_ref[k].astype(f32) for k in range(got_ref.shape[0]))


def tally(got):
    return call(tally_kernel, 8, shape(got.shape[1:], f32), 1_000_000_000, 1_500_000)(got)


def finish_kernel(got_ref, proj_ref, router_ref, gain_ref):
    total = sum(got_ref[k] for k in range(got_ref.shape[0]))
    step = SHARE_ROWS // 4
    lane = iota((1, 4), 1)
    gain = jnp.zeros((1, 4), f32)
    for r in range(4):
        for s in range(BLOCKS):
            proj_ref[r : r + 1, s * LANES : (s + 1) * LANES] = total[r * step + s : r * step + s + 1]
        at = r * step + BLOCKS
        extra = total[at : at + 1] + total[at + 1 : at + 2]
        router_ref[r : r + 1, :] = extra[:, :EXPERTS]
        gain = jnp.where(lane == r, extra[:, EXPERTS : EXPERTS + 1], gain)
    gain_ref[...] = gain


def finish(got):
    return call(
        finish_kernel,
        4,
        (shape((4, D), f32), shape((4, EXPERTS), f32), shape((1, 4), f32)),
        1_000_000_000,
        200_000,
    )(got)


def swap(value, step):
    return lax.ppermute(value, "lat", [(k, k ^ step) for k in range(4)])


def exchange(value, axes="lon", groups=None):
    return lax.all_to_all(
        value, axes, split_axis=0, concat_axis=0, tiled=True, axis_index_groups=groups
    )


def spread(value):
    return exchange(value.reshape(EXPERTS, -1, LANES)).reshape(-1, LANES)


RING = 8
ALONG = [[line * RING + k for k in range(RING)] for line in range(EXPERTS // RING)]
ACROSS = [
    [
        (2 * row + core) * EXPERTS + line * RING + k
        for row in range(2)
        for line in range(EXPERTS // RING)
    ]
    for core in range(2)
    for k in range(RING)
]


KEYS = 64
GROUPS = D // LANES
PER = LANES // (D // NH)
SPAN = 40
LINES = 32


def head_masks(kind):
    lane = iota((KEYS, LANES), 1) // (D // NH)
    return [jnp.where(lane == j, 1.0, 0.0).astype(kind) for j in range(PER)]


def by_head(values, masks):
    return jnp.concatenate([values * mask for mask in masks], axis=0)


def halves(values, pick):
    first = iota(values.shape, 1) < KEYS
    left = pick(values, first)
    right = pick(values, jnp.logical_not(first))
    return jnp.where(first, left, right)


def half_sum(values):
    return halves(
        values, lambda v, m: jnp.sum(jnp.where(m, v, 0.0), axis=-1, keepdims=True)
    )


def half_max(values):
    return halves(
        values, lambda v, m: jnp.max(jnp.where(m, v, -3e38), axis=-1, keepdims=True)
    )


def attend_kernel(
    shift_ref, left_ref, own_ref, right_ref, *refs
):
    saved, (att_ref, wide, win, back, flat) = (refs[:8], refs[8:])
    shifted = shift_ref[0]
    factor = (D // NH) ** (-0.5)
    for row in range(ROWS_DEV):
        for i in range(3):
            line = row * 3 + i
            wide[line, COLS_DEV + 2 * WIN - 3 : SPAN, :] = jnp.zeros((8, D), f32)
            wide[line, :WIN, :] = left_ref[row, i].astype(f32)
            wide[line, WIN : WIN + COLS_DEV, :] = own_ref[row, i].astype(f32)
            wide[line, WIN + COLS_DEV : 2 * WIN + COLS_DEV, :] = right_ref[row, i].astype(f32)
            turned = pltpu.roll(wide[line], SPAN - WIN + shifted, 0)
            wide[line] = turned
            for w in range(4):
                win[i, w, row * 8 : (row + 1) * 8, :] = wide[line, WIN * w : WIN * w + 8, :]
    win[:, :, KEYS - 8 :, :] = jnp.zeros((3, 4, 8, D), f32)
    masks = head_masks(bf16)
    key = iota((KEYS, LANES), 1) & (KEYS - 1)
    real = (key < ROWS_DEV * 8) & ((key & 7) < WIN)

    def window(outer, at_w, carry):
        q_ref, k_ref, v_ref, p_ref = saved[4 * outer : 4 * outer + 4]
        w = 3 * at_w if outer else at_w + 1
        q_ref[at_w] = win[0, w].astype(bf16)
        k_ref[at_w] = win[1, w].astype(bf16)
        v_ref[at_w] = win[2, w].astype(bf16)
        for block in range(GROUPS):
            at = slice(block * LANES, (block + 1) * LANES)
            keys = by_head(k_ref[at_w, :, at], masks)
            values = by_head(v_ref[at_w, :, at], masks)
            scores = mm_cols(q_ref[at_w, :, at], keys) * factor
            parts = []
            for half in range(2):
                held = jnp.where(real, scores[:, half * LANES : (half + 1) * LANES], -1e30)
                raised = jnp.exp(held - half_max(held))
                probs = raised / half_sum(raised)
                base = (2 * block + half) * LANES
                p_ref[at_w, :, base : base + LANES] = probs
                parts.append(probs.astype(bf16))
            win[0, w, :, at] = mm(jnp.concatenate(parts, axis=1), values)
        return carry

    for outer in range(2):
        lax.fori_loop(0, 2, functools.partial(window, outer), 0)
    flat[...] = jnp.zeros_like(flat)
    for row in range(ROWS_DEV):
        for w in range(4):
            back[row, WIN * w : WIN * w + 8, :] = win[0, w, row * 8 : (row + 1) * 8, :]
        turned = pltpu.roll(back[row], jnp.where(shifted == 0, 0, LINES - shifted), 0)
        flat[row * PITCH : row * PITCH + COLS_DEV, :] = turned[:COLS_DEV]
    att_ref[...] = flat[...].astype(bf16)


def attend(shifted, left, own, right):
    inner = pl.BlockSpec(memory_space=pltpu.VMEM)
    return call(
        attend_kernel,
        56,
        (
            *(3 * [shape((2, KEYS, D), bf16)] + [shape((2, KEYS, 2 * D), f32)]) * 2,
            shape((PAY_ROWS, D), bf16),
        ),
        18_000_000_000,
        6_000_000,
        [
            pltpu.VMEM((3 * ROWS_DEV, SPAN, D), f32),
            pltpu.VMEM((3, 4, KEYS, D), f32),
            pltpu.VMEM((ROWS_DEV, LINES, D), f32),
            pltpu.VMEM((PAY_ROWS, D), f32),
        ],
        in_specs=[pl.BlockSpec(memory_space=pltpu.SMEM)] + [inner] * 3,
    )(shifted, left, own, right)


def attend_grad_kernel(
    outer, shift_ref, own_ref, q_ref, k_ref, v_ref, p_ref, *refs
):
    shifted = shift_ref[0]
    if outer:
        left_ref, right_ref, done_ref, out_ref, wide, win, back = refs
        win[:, 1:3] = done_ref[...].astype(f32)
        windows = (0, 3)
    else:
        out_ref, wide, win = refs
        windows = (1, 2)
    factor = (D // NH) ** (-0.5)
    valid = jnp.where(iota((8, 1), 0) < WIN, 1.0, 0.0)
    for row in range(ROWS_DEV):
        wide[row, COLS_DEV + 2 * WIN - 3 : SPAN, :] = jnp.zeros((8, D), f32)
        wide[row, WIN : WIN + COLS_DEV, :] = own_ref[row].astype(f32)
        if outer:
            wide[row, :WIN, :] = left_ref[row].astype(f32)
            wide[row, WIN + COLS_DEV : 2 * WIN + COLS_DEV, :] = right_ref[row].astype(f32)
        else:
            wide[row, :WIN, :] = jnp.zeros((WIN, D), f32)
            wide[row, WIN + COLS_DEV : 2 * WIN + COLS_DEV, :] = jnp.zeros((WIN, D), f32)
        wide[row] = pltpu.roll(wide[row], SPAN - WIN + shifted, 0)
        for w in windows:
            win[0, w, row * 8 : (row + 1) * 8, :] = wide[row, WIN * w : WIN * w + 8, :] * valid
    for w in windows:
        win[0, w, KEYS - 8 :, :] = jnp.zeros((8, D), f32)
    masks = head_masks(bf16)
    wide_masks = head_masks(f32)

    def gathered(values):
        return sum(
            wide_masks[j] * values[j * KEYS : (j + 1) * KEYS] for j in range(PER)
        )

    def window(at_w, carry):
        w = 3 * at_w if outer else at_w + 1
        for block in range(GROUPS):
            at = slice(block * LANES, (block + 1) * LANES)
            upstream = win[0, w, :, at].astype(bf16)
            keys = by_head(k_ref[at_w, :, at], masks)
            values = by_head(v_ref[at_w, :, at], masks)
            grad_probs = mm_cols(upstream, values)
            low = []
            grads = []
            for half in range(2):
                base = (2 * block + half) * LANES
                probs = p_ref[at_w, :, base : base + LANES]
                part = grad_probs[:, half * LANES : (half + 1) * LANES]
                grads.append((probs * (part - half_sum(part * probs)) * factor).astype(bf16))
                low.append(probs.astype(bf16))
            grad_scores = jnp.concatenate(grads, axis=1)
            win[0, w, :, at] = mm(grad_scores, keys)
            win[1, w, :, at] = gathered(mm_rows(grad_scores, q_ref[at_w, :, at]))
            win[2, w, :, at] = gathered(mm_rows(jnp.concatenate(low, axis=1), upstream))
        return carry

    lax.fori_loop(0, 2, window, 0)
    if not outer:
        out_ref[...] = win[:, 1:3].astype(bf16)
        return
    for row in range(ROWS_DEV):
        for i in range(3):
            line = row * 3 + i
            for w in range(4):
                back[line, WIN * w : WIN * w + 8, :] = win[i, w, row * 8 : (row + 1) * 8, :]
            turned = pltpu.roll(back[line], jnp.where(shifted == 0, 0, LINES - shifted), 0)
            out_ref[row, i] = turned[:COLS_DEV].astype(bf16)


def attend_grad(shifted, own, saved, edges=()):
    inner = pl.BlockSpec(memory_space=pltpu.VMEM)
    part = shape((3, 2, KEYS, D), bf16)
    scratch = [pltpu.VMEM((ROWS_DEV, SPAN, D), f32), pltpu.VMEM((3, 4, KEYS, D), f32)]
    if edges:
        part = shape((ROWS_DEV, 3, COLS_DEV, D), bf16)
        scratch.append(pltpu.VMEM((3 * ROWS_DEV, LINES, D), f32))
    return call(
        functools.partial(attend_grad_kernel, bool(edges)),
        56,
        part,
        10_000_000_000,
        6_000_000,
        scratch,
        in_specs=[pl.BlockSpec(memory_space=pltpu.SMEM)] + [inner] * (5 + len(edges)),
    )(shifted, own, *saved, *edges)


def halo(values, axis):
    count = lax.axis_size("lon")
    length = values.shape[axis]
    left = lax.ppermute(
        lax.slice_in_dim(values, length - WIN, length, axis=axis),
        "lon",
        [(i, (i + 1) % count) for i in range(count)],
    )
    right = lax.ppermute(
        lax.slice_in_dim(values, 0, WIN, axis=axis),
        "lon",
        [((i + 1) % count, i) for i in range(count)],
    )
    return (left, values, right)


def shards(
    resid, qkv, out_proj, norm_gain, router, w_in, w_out, expert_ids, slots, shifts, grad_out
):
    lat = lax.axis_index("lat")
    lon = lax.axis_index("lon")
    router_t = router.T
    gain = norm_gain.reshape(1, D)
    places = (expert_ids.transpose(0, 2, 1), slots.transpose(0, 2, 1))
    send, split_router, routed_in, normed, stats, back_at = front(
        resid, grad_out, gain, router_t, *places
    )
    shifted = shifts[lat].reshape(1)
    own = unfold(spread(send))
    own, qkv = lax.optimization_barrier((own, qkv))
    left, here, right = halo(qkv.transpose(0, 2, 1, 3), 2)
    far = [swap(part, 2) for part in own]
    near = [swap(part, 1) for part in own]

    expert = lon.astype(jnp.int32).reshape(1)
    weights = (w_in[0], w_out[0], split_router)
    chunks = [*own, *near]
    dx_own, dx_near, cu, dh = experts(expert, chunks, *weights)
    cus, dhs, far_sums = ([cu], [dh], [])
    far[0], dx_own = lax.optimization_barrier((far[0], dx_own))
    near_sum = swap(dx_near, 1)
    for part in range(2):
        pair = [far[part], swap(far[part], 1)]
        if part == 1:
            *pair, pair_sum = lax.optimization_barrier((*pair, pair_sum))
            far_sums.append(swap(pair_sum, 2))
        dx_far, dx_cross, cu, dh = experts(expert, pair, *weights)
        if part == 0:
            far[1], dx_far, dx_cross = lax.optimization_barrier((far[1], dx_far, dx_cross))
            dx_cross = swap(dx_cross, 1)
        else:
            dx_cross, far_sums[0], left, right = lax.optimization_barrier(
                (swap(dx_cross, 1), far_sums[0], left, right)
            )
        pair_sum = (dx_far.astype(f32) + dx_cross.astype(f32)).astype(bf16)
        chunks += pair
        cus.append(cu)
        dhs.append(dh)
    far_sums.append(swap(pair_sum, 2))
    folded = fold(dx_own, near_sum, *far_sums)
    folded, chunks, cus, left, right = lax.optimization_barrier((folded, chunks, cus, left, right))
    back = spread(folded)
    *saved, attended = attend(shifted, left, here, right)
    core = lat & 1

    def side_for(core):
        return jnp.concatenate(
            [
                lax.dynamic_slice_in_dim(values, (2 * block + core) * QUARTER, QUARTER, 1)
                for values in (routed_in, attended)
                for block in range(2)
            ],
            axis=1,
        )

    sides = (side_for(core), swap(side_for(1 - core), 1))
    all_grad = jnp.concatenate([chunk[chunk.shape[0] // 2 :] for chunk in chunks], axis=0)
    d_w_out = mm_rows(jnp.concatenate(cus, axis=0), all_grad).astype(bf16)
    back, sides, d_w_out = lax.optimization_barrier((back, sides, d_w_out))
    d_resid, d_attn, pay = middle(
        back, back_at, normed, stats, grad_out, gain, router_t, out_proj
    )
    shares = share(core.astype(jnp.int32).reshape(1), pay, swap(pay, 1), *sides)
    shares, d_attn, chunks, dhs = lax.optimization_barrier((shares, d_attn, chunks, dhs))
    left, d_attn, right = halo(d_attn, 1)
    inside = attend_grad(shifted, d_attn, saved[:4])
    all_in = jnp.concatenate([chunk[: chunk.shape[0] // 2] for chunk in chunks], axis=0)
    d_w_in = mm_rows(all_in, jnp.concatenate(dhs, axis=0)).astype(bf16)
    shares = shares.reshape(2 * RING, RING * SHARE_ROWS, LANES)
    shares = exchange(shares, ("lat", "lon"), ACROSS)
    shares, inside, d_w_in = lax.optimization_barrier((shares, inside, d_w_in))
    shares = tally(shares).reshape(RING, SHARE_ROWS, LANES)
    left, right, shares = lax.optimization_barrier((left, right, shares))
    d_qkv = attend_grad(shifted, d_attn, saved[4:], (left, right, inside)).transpose(0, 2, 1, 3)
    proj_share, router_share, gain_share = finish(exchange(shares, groups=ALONG))
    return (
        d_resid,
        d_qkv,
        proj_share,
        gain_share.reshape(4),
        router_share,
        d_w_in[None],
        d_w_out[None],
    )


def solution(mesh):
    in_specs = (
        P("lat", "lon", None),
        P("lat", "lon", None, None),
        P(),
        P(),
        P(),
        P("lon", None, "lat"),
        P("lon", "lat", None),
        P("lat", "lon", None),
        P("lat", "lon", None),
        P(),
        P("lat", "lon", None),
    )
    out_specs = (
        P("lat", "lon", None),
        P("lat", "lon", None, None),
        P(("lat", "lon"), None),
        P(("lat", "lon")),
        P(("lat", "lon"), None),
        P("lon", None, "lat"),
        P("lon", "lat", None),
    )
    return jax.shard_map(shards, mesh=mesh, in_specs=in_specs, out_specs=out_specs, check_vma=False)
```

```python
import functools

import jax
import jax.numpy as jnp
from jax import lax
from jax.experimental import pallas as pl
from jax.experimental.pallas import tpu as pltpu
from jax.sharding import PartitionSpec as P

D = 1024
NH = 32
WIN = 7
ROWS_DEV = 7
COLS_DEV = 21
PITCH = 24
TOK = ROWS_DEV * PITCH
EXPERTS = 64
CAP = 5
LANES = 128
BLOCKS = D // LANES
SLOTS = EXPERTS * CAP
SEND_ROWS = 2 * CAP * BLOCKS
BACK_ROWS = CAP * BLOCKS + 8
SHARE_ROWS = 40
PAY_ROWS = TOK + 8
WIDE = D + LANES

norm_eps = 1e-05
zloss_weight = 0.25
bf16 = jnp.bfloat16
f32 = jnp.float32
MEBI = 1024 * 1024


def call(kernel, vmem, out_shape, flops, moved, scratch=(), **kwargs):
    return pl.pallas_call(
        kernel,
        out_shape=out_shape,
        scratch_shapes=list(scratch),
        compiler_params=pltpu.CompilerParams(vmem_limit_bytes=vmem * MEBI),
        cost_estimate=pl.CostEstimate(flops=flops, bytes_accessed=moved, transcendentals=0),
        **kwargs,
    )


def mm(left, right):
    return lax.dot_general(left, right, (((1,), (0,)), ((), ())), preferred_element_type=f32)


def mm_cols(left, right):
    return lax.dot_general(left, right, (((1,), (1,)), ((), ())), preferred_element_type=f32)


def mm_rows(left, right):
    return lax.dot_general(left, right, (((0,), (0,)), ((), ())), preferred_element_type=f32)


def shape(dims, kind):
    return jax.ShapeDtypeStruct(dims, kind)


def iota(dims, axis):
    return lax.broadcasted_iota(jnp.int32, dims, axis)


def split3(value):
    high = value.astype(bf16)
    rest = value - high.astype(f32)
    middle = rest.astype(bf16)
    return (high, middle, (rest - middle.astype(f32)).astype(bf16))


def softmax_parts(logits):
    held = jnp.where(iota(logits.shape, 1) < EXPERTS, logits, -1e30)
    top = jnp.max(held, axis=-1, keepdims=True)
    raised = jnp.exp(held - top)
    total = jnp.sum(raised, axis=-1, keepdims=True)
    return (raised / total, top + jnp.log(total))


def three_logits(rows, split_router):
    triple = mm_cols(rows, split_router)
    return triple[:, 2 * LANES :] + triple[:, LANES : 2 * LANES] + triple[:, :LANES]


def front_kernel(
    resid_ref, grad_ref, gain_ref, router_ref, ids_ref, slots_ref,
    send_ref, split_ref, z_ref, normed_ref, stats_ref, back_ref, rows, folded, target_ref,
):
    target_ref[...] = jnp.full((2, 2 * TOK), -1, jnp.int32)
    back_ref[...] = jnp.full((2, TOK), -1, jnp.int32)
    for row in range(ROWS_DEV):
        ids = ids_ref[row]
        spots = slots_ref[row]
        base = row * PITCH
        back_ref[:, base : base + COLS_DEV] = spots * EXPERTS + ids
        target_ref[:, base : base + COLS_DEV] = ids * (2 * CAP) + spots
        target_ref[:, TOK + base : TOK + base + COLS_DEV] = ids * (2 * CAP) + spots + CAP
    rows[...] = jnp.zeros_like(rows)
    for row in range(ROWS_DEV):
        rows[row * PITCH : row * PITCH + COLS_DEV, :] = resid_ref[row].astype(f32)
        base = TOK + row * PITCH
        rows[base : base + COLS_DEV, :] = grad_ref[row].astype(f32)
    resid = rows[:TOK, :]
    center = resid - jnp.mean(resid, axis=-1, keepdims=True)
    inv_std = lax.rsqrt(jnp.mean(center * center, axis=-1, keepdims=True) + norm_eps)
    normed = center * inv_std
    normed_ref[...] = normed
    rows[:TOK, :] = normed * gain_ref[...]
    both = rows[...].astype(bf16)
    slot = iota((2 * SLOTS, 2 * TOK), 0)
    pick = jnp.where(
        (slot == target_ref[0:1, :]) | (slot == target_ref[1:2, :]), 1.0, 0.0
    ).astype(bf16)
    for pair in range(BLOCKS // 2):
        got = mm(pick, both[:, pair * 2 * LANES : (pair + 1) * 2 * LANES])
        for half in range(2):
            folded[pl.ds(2 * pair + half, 2 * SLOTS, stride=BLOCKS), :] = got[
                :, half * LANES : (half + 1) * LANES
            ]
    send_ref[...] = folded[...].astype(bf16)
    empty = jnp.zeros((LANES - EXPERTS, D), bf16)
    for index, part in enumerate(split3(router_ref[...])):
        split_ref[index * LANES : index * LANES + EXPERTS, :] = part
        split_ref[index * LANES + EXPERTS : (index + 1) * LANES, :] = empty
    z_ref[...] = jnp.where(iota((PAY_ROWS, 1), 0) < TOK, rows[:PAY_ROWS, :], 0.0).astype(bf16)
    probs, log_total = softmax_parts(three_logits(both[:PAY_ROWS, :], split_ref[...]))
    stats_ref[:, :LANES] = probs[:TOK]
    stats_ref[:, LANES : 2 * LANES] = jnp.broadcast_to(log_total[:TOK], (TOK, LANES))
    stats_ref[:, 2 * LANES :] = jnp.broadcast_to(inv_std, (TOK, LANES))


def front(resid, grad, gain, router_t, ids, slots):
    return call(
        front_kernel,
        56,
        (
            shape((EXPERTS * SEND_ROWS, LANES), bf16),
            shape((3 * LANES, D), bf16),
            shape((PAY_ROWS, D), bf16),
            shape((TOK, D), f32),
            shape((TOK, 3 * LANES), f32),
            shape((2, TOK), jnp.int32),
        ),
        4_600_000_000,
        4_000_000,
        [
            pltpu.VMEM((2 * TOK, D), f32),
            pltpu.VMEM((EXPERTS * SEND_ROWS, LANES), f32),
            pltpu.VMEM((2, 2 * TOK), jnp.int32),
        ],
    )(resid, grad, gain, router_t, ids, slots)


PARTS = (3 * EXPERTS, 2 * EXPERTS)


def unfold_kernel(got_ref, first_ref, second_ref, wide):
    wide[...] = got_ref[...].astype(f32)
    for c in range(2 * CAP):
        ref, place = (first_ref, c % CAP) if c % CAP < 3 else (second_ref, c % CAP - 3)
        base = place * EXPERTS + (c // CAP) * ref.shape[0] // 2
        for s in range(BLOCKS):
            ref[base : base + EXPERTS, s * LANES : (s + 1) * LANES] = wide[
                pl.ds(c * BLOCKS + s, EXPERTS, stride=SEND_ROWS), :
            ].astype(bf16)


def unfold(got):
    return call(
        unfold_kernel,
        14,
        tuple(shape((2 * part, D), bf16) for part in PARTS),
        3_900_000_000,
        2_600_000,
        [pltpu.VMEM((EXPERTS * SEND_ROWS, LANES), f32)],
    )(got)


FF_TILE = 256


def expert_kernel(count, expert_ref, *refs):
    chunks = refs[:count]
    in_ref, out_w_ref, split_ref, near_ref, far_ref, cu_ref, dh_ref = refs[count : count + 7]
    inputs, grads, total, dc, comb = refs[count + 7 :]
    step = pl.program_id(0)
    rows = inputs.shape[0]

    @pl.when(step == 0)
    def _():
        base = 0
        for ref in chunks:
            part = ref.shape[0] // 2
            inputs[base : base + part, :] = ref[:part, :]
            grads[base : base + part, :] = ref[part:, :]
            base += part
        probs, _unused = softmax_parts(three_logits(inputs[...], split_ref[...]))
        mine = jnp.where(iota(probs.shape, 1) == expert_ref[0], probs, 0.0)
        weight = jnp.sum(mine, axis=-1, keepdims=True).astype(bf16).astype(f32)
        comb[...] = jnp.broadcast_to(weight, (rows, LANES))
        dc[...] = jnp.zeros_like(dc)
        total[...] = jnp.zeros_like(total)

    weight_in = in_ref[...]
    hidden = mm(inputs[...], weight_in)
    grad_w = mm_cols(grads[...], out_w_ref[...])
    cdf = 0.5 * (1.0 + lax.erf(hidden * 0.7071067811865476))
    active = hidden * cdf
    slope = cdf + hidden * jnp.exp(-0.5 * hidden * hidden) * 0.3989422804014327
    dc[...] += jnp.broadcast_to(jnp.sum(active * grad_w, axis=-1, keepdims=True), (rows, LANES))
    weight = comb[:, 0:1]
    cu_ref[...] = (weight * active).astype(bf16)
    grad_hidden = (weight * grad_w * slope).astype(bf16)
    dh_ref[...] = grad_hidden
    total[...] += mm_cols(grad_hidden, weight_in)

    @pl.when(step == pl.num_programs(0) - 1)
    def _():
        for index, ref in enumerate((near_ref, far_ref)):
            span = slice(index * rows // 2, (index + 1) * rows // 2)
            ref[:, :D] = total[span, :].astype(bf16)
            ref[:, D:] = dc[span, :].astype(bf16)


def experts(expert, chunks, weight_in, weight_out, split_router):
    width = weight_in.shape[1]
    count = len(chunks)
    rows = sum(chunk.shape[0] for chunk in chunks) // 2
    whole = lambda dims: pl.BlockSpec(dims, lambda j: (0,) * len(dims))
    return call(
        functools.partial(expert_kernel, count),
        56 if count == 4 else 30,
        (
            shape((rows // 2, WIDE), bf16),
            shape((rows // 2, WIDE), bf16),
            shape((rows, width), bf16),
            shape((rows, width), bf16),
        ),
        22 * rows * D * width,
        12_000_000,
        [
            pltpu.VMEM((rows, D), bf16),
            pltpu.VMEM((rows, D), bf16),
            pltpu.VMEM((rows, D), f32),
            pltpu.VMEM((rows, LANES), f32),
            pltpu.VMEM((rows, LANES), f32),
        ],
        grid=(width // FF_TILE,),
        in_specs=[pl.BlockSpec(memory_space=pltpu.SMEM)]
        + [whole(chunk.shape) for chunk in chunks]
        + [
            pl.BlockSpec((D, FF_TILE), lambda j: (0, j)),
            pl.BlockSpec((FF_TILE, D), lambda j: (j, 0)),
            whole((3 * LANES, D)),
        ],
        out_specs=(
            whole((rows // 2, WIDE)),
            whole((rows // 2, WIDE)),
            pl.BlockSpec((rows, FF_TILE), lambda j: (0, j)),
            pl.BlockSpec((rows, FF_TILE), lambda j: (0, j)),
        ),
    )(expert, *chunks, weight_in, weight_out, split_router)


def weight_kernel(count, *refs):
    left, right, (out_ref, left_rows, right_rows) = (refs[:count], refs[count:-3], refs[-3:])

    def gather(parts, stack):
        base = 0
        for ref in parts:
            stack[base : base + ref.shape[0], :] = ref[...]
            base += ref.shape[0]

    @pl.when(pl.program_id(0) == 0)
    def _():
        gather(right, right_rows)

    gather(left, left_rows)
    out_ref[...] = mm_rows(left_rows[...], right_rows[...]).astype(bf16)


def weight_grad(left, right):
    block = 256

    def rows(pair):
        return pair[0].shape[0] // (1 if pair[1] is None else 2)

    def spec(pair, wide):
        half = pair[1] or 0
        if wide:
            return pl.BlockSpec((rows(pair), D), lambda j: (half, 0))
        return pl.BlockSpec((rows(pair), block), lambda j: (half, j))

    total = sum(rows(pair) for pair in left)
    return call(
        functools.partial(weight_kernel, len(left)),
        32,
        shape((D, D), bf16),
        1_000_000,
        1_000_000,
        [pltpu.VMEM((total, block), bf16), pltpu.VMEM((total, D), bf16)],
        grid=(D // block,),
        in_specs=[spec(pair, False) for pair in left] + [spec(pair, True) for pair in right],
        out_specs=pl.BlockSpec((block, D), lambda j: (j, 0)),
    )(*[pair[0] for pair in left], *[pair[0] for pair in right])


def fold_kernel(own_ref, near_ref, first_ref, second_ref, out_ref, folded, total):
    total[...] = own_ref[...].astype(f32) + near_ref[...].astype(f32)
    total[: PARTS[0], :] += first_ref[...].astype(f32)
    total[PARTS[0] :, :] += second_ref[...].astype(f32)
    for c in range(CAP):
        part = total[c * EXPERTS : (c + 1) * EXPERTS, :]
        for s in range(BLOCKS):
            folded[pl.ds(c * BLOCKS + s, EXPERTS, stride=BACK_ROWS), :] = part[
                :, s * LANES : (s + 1) * LANES
            ]
        folded[pl.ds(CAP * BLOCKS + c, EXPERTS, stride=BACK_ROWS), :] = part[:, D:]
    for spare in range(CAP * BLOCKS + CAP, BACK_ROWS):
        folded[pl.ds(spare, EXPERTS, stride=BACK_ROWS), :] = jnp.zeros((EXPERTS, LANES), f32)
    out_ref[...] = folded[...].astype(bf16)


def fold(own, near, first, second):
    return call(
        fold_kernel,
        14,
        shape((EXPERTS * BACK_ROWS, LANES), bf16),
        3_800_000_000,
        3_000_000,
        [pltpu.VMEM((EXPERTS * BACK_ROWS, LANES), f32), pltpu.VMEM((SLOTS, WIDE), f32)],
    )(own, near, first, second)


def middle_kernel(
    back_ref, target_ref, normed_ref, stats_ref, grad_ref, gain_ref, router_ref, proj_ref,
    resid_ref, attn_ref, pay_ref, wide, table, rows,
):
    wide[...] = back_ref[...].astype(f32)
    lane = iota((EXPERTS, LANES), 1)
    same = lane == iota((EXPERTS, LANES), 0)
    for c in range(CAP):
        span = slice(c * EXPERTS, (c + 1) * EXPERTS)
        for s in range(BLOCKS):
            table[span, s * LANES : (s + 1) * LANES] = wide[
                pl.ds(c * BLOCKS + s, EXPERTS, stride=BACK_ROWS), :
            ].astype(bf16)
        weights = wide[pl.ds(CAP * BLOCKS + c, EXPERTS, stride=BACK_ROWS), :]
        table[span, D:] = jnp.where(same, weights, 0.0).astype(bf16)
    slot = iota((SLOTS, TOK), 0)
    pick = jnp.where(
        (slot == target_ref[0:1, :]) | (slot == target_ref[1:2, :]), 1.0, 0.0
    ).astype(bf16)
    routed = mm_rows(pick, table[...])
    grad_probs = routed[:, D:]
    probs = stats_ref[:, :LANES]
    log_total = stats_ref[:, LANES : 2 * LANES]
    inv_std = stats_ref[:, 2 * LANES : 2 * LANES + 1]
    grad_logits = (
        probs * (grad_probs - jnp.sum(probs * grad_probs, axis=-1, keepdims=True))
        + 2.0 * zloss_weight * log_total * probs
    )
    grad_z = routed[:, :D] + jnp.dot(
        grad_logits[:, :EXPERTS], router_ref[...], precision=lax.Precision.HIGHEST,
        preferred_element_type=f32,
    )
    normed = normed_ref[...]
    gain_term = jnp.sum(grad_z * normed, axis=0, keepdims=True)
    rows[...] = jnp.zeros_like(rows)
    for row in range(ROWS_DEV):
        rows[row * PITCH : row * PITCH + COLS_DEV, :] = grad_ref[row].astype(f32)
    grad_normed = grad_z * gain_ref[...]
    rows[:TOK, :] = rows[:TOK, :] + inv_std * (
        grad_normed
        - jnp.mean(grad_normed, axis=-1, keepdims=True)
        - normed * jnp.mean(grad_normed * normed, axis=-1, keepdims=True)
    )
    for row in range(ROWS_DEV):
        resid_ref[row] = rows[row * PITCH : row * PITCH + COLS_DEV, :].astype(bf16)
    low = rows[...].astype(bf16)
    rows[...] = mm_cols(low, proj_ref[...])
    for row in range(ROWS_DEV):
        attn_ref[row] = rows[row * PITCH : row * PITCH + COLS_DEV, :].astype(bf16)
    high, middle, last = (part.astype(f32) for part in split3(gain_term))
    extra = iota((PAY_ROWS, 1), 0)
    rows[...] = jnp.where(
        extra < TOK,
        low.astype(f32),
        jnp.where(
            extra == TOK, high, jnp.where(extra == TOK + 1, middle, jnp.where(extra == TOK + 2, last, 0.0))
        ),
    )
    pay_ref[:, :D] = rows[...].astype(bf16)
    upper = grad_logits.astype(bf16).astype(f32)
    lower = (grad_logits - upper).astype(bf16).astype(f32)
    mixed = upper + pltpu.roll(lower, EXPERTS, 1)
    pay_ref[:, D:] = jnp.concatenate([mixed, jnp.zeros((PAY_ROWS - TOK, LANES), f32)], axis=0).astype(bf16)


def middle(back, targets, normed, stats, grad, gain, router_t, out_proj):
    return call(
        middle_kernel,
        56,
        (
            shape((ROWS_DEV, COLS_DEV, D), bf16),
            shape((ROWS_DEV, COLS_DEV, D), bf16),
            shape((PAY_ROWS, WIDE), bf16),
        ),
        7_000_000_000,
        6_000_000,
        [
            pltpu.VMEM((EXPERTS * BACK_ROWS, LANES), f32),
            pltpu.VMEM((SLOTS, WIDE), bf16),
            pltpu.VMEM((PAY_ROWS, D), f32),
        ],
    )(back, targets, normed, stats, grad, gain, router_t, out_proj)


SHARED = EXPERTS * SHARE_ROWS
QUARTER = D // 4


def share_kernel(core_ref, pay_ref, pay_near_ref, side_ref, side_near_ref, out_ref, folded):
    both = ((pay_ref, side_ref), (pay_near_ref, side_near_ref))
    gain = jnp.zeros((1, D), f32)
    at = iota((16, 1), 0)
    for pay, _unused in both:
        last = pay[PAY_ROWS - 16 :, :D].astype(f32)
        gain += jnp.sum(jnp.where((at >= 8) & (at < 11), last, 0.0), axis=0, keepdims=True)
    same = iota((QUARTER, QUARTER), 0) == iota((QUARTER, QUARTER), 1)
    lane = iota((QUARTER, LANES), 1)
    step = SHARE_ROWS // 4
    for block in range(2):
        z_at = slice(block * QUARTER, (block + 1) * QUARTER)
        a_at = slice((2 + block) * QUARTER, (3 + block) * QUARTER)
        proj = sum(mm_rows(side[:, a_at], pay[:, :D]) for pay, side in both)
        router = sum(mm_rows(side[:, z_at], pay[:, D:]) for pay, side in both)
        mine = jnp.zeros((1, QUARTER), f32)
        for core in range(2):
            place = (2 * block + core) * QUARTER
            mine += jnp.where(core_ref[0] == core, gain[:, place : place + QUARTER], 0.0)
        column = jnp.sum(jnp.where(same, mine, 0.0), axis=-1, keepdims=True)
        router = router + pltpu.roll(router, EXPERTS, 1)
        extra = jnp.where(lane < EXPERTS, router, jnp.where(lane == EXPERTS, column, 0.0))
        upper = extra.astype(bf16).astype(f32)
        base = block * SHARED
        for s in range(BLOCKS):
            folded[pl.ds(base + s, QUARTER, stride=step), :] = proj[:, s * LANES : (s + 1) * LANES]
        folded[pl.ds(base + BLOCKS, QUARTER, stride=step), :] = upper
        folded[pl.ds(base + BLOCKS + 1, QUARTER, stride=step), :] = extra - upper
    out_ref[...] = folded[...].astype(bf16)


def share(core, *arrays):
    inner = pl.BlockSpec(memory_space=pltpu.VMEM)
    return call(
        share_kernel,
        20,
        shape((2 * SHARED, LANES), bf16),
        3_900_000_000,
        4_000_000,
        [pltpu.VMEM((2 * SHARED, LANES), f32)],
        in_specs=[pl.BlockSpec(memory_space=pltpu.SMEM)] + [inner] * 4,
    )(core, *arrays)


def tally_kernel(got_ref, out_ref):
    out_ref[...] = sum(got_ref[k].astype(f32) for k in range(got_ref.shape[0]))


def tally(got):
    return call(tally_kernel, 8, shape(got.shape[1:], f32), 1_000_000_000, 1_500_000)(got)


def finish_kernel(got_ref, proj_ref, router_ref, gain_ref):
    total = sum(got_ref[k] for k in range(got_ref.shape[0]))
    step = SHARE_ROWS // 4
    lane = iota((1, 4), 1)
    gain = jnp.zeros((1, 4), f32)
    for r in range(4):
        for s in range(BLOCKS):
            proj_ref[r : r + 1, s * LANES : (s + 1) * LANES] = total[r * step + s : r * step + s + 1]
        at = r * step + BLOCKS
        extra = total[at : at + 1] + total[at + 1 : at + 2]
        router_ref[r : r + 1, :] = extra[:, :EXPERTS]
        gain = jnp.where(lane == r, extra[:, EXPERTS : EXPERTS + 1], gain)
    gain_ref[...] = gain


def finish(got):
    return call(
        finish_kernel,
        4,
        (shape((4, D), f32), shape((4, EXPERTS), f32), shape((1, 4), f32)),
        1_000_000_000,
        200_000,
    )(got)


def swap(value, step):
    return lax.ppermute(value, "lat", [(k, k ^ step) for k in range(4)])


def exchange(value, axes="lon", groups=None):
    return lax.all_to_all(
        value, axes, split_axis=0, concat_axis=0, tiled=True, axis_index_groups=groups
    )


def spread(value):
    return exchange(value.reshape(EXPERTS, -1, LANES)).reshape(-1, LANES)


RING = 8
ALONG = [[line * RING + k for k in range(RING)] for line in range(EXPERTS // RING)]
ACROSS = [
    [
        (2 * row + core) * EXPERTS + line * RING + k
        for row in range(2)
        for line in range(EXPERTS // RING)
    ]
    for core in range(2)
    for k in range(RING)
]


KEYS = 64
GROUPS = D // LANES
PER = LANES // (D // NH)
SPAN = 40
LINES = 32


def head_masks(kind):
    lane = iota((KEYS, LANES), 1) // (D // NH)
    return [jnp.where(lane == j, 1.0, 0.0).astype(kind) for j in range(PER)]


def by_head(values, masks):
    return jnp.concatenate([values * mask for mask in masks], axis=0)


def halves(values, pick):
    first = iota(values.shape, 1) < KEYS
    left = pick(values, first)
    right = pick(values, jnp.logical_not(first))
    return jnp.where(first, left, right)


def half_sum(values):
    return halves(
        values, lambda v, m: jnp.sum(jnp.where(m, v, 0.0), axis=-1, keepdims=True)
    )


def half_max(values):
    return halves(
        values, lambda v, m: jnp.max(jnp.where(m, v, -3e38), axis=-1, keepdims=True)
    )


def attend_kernel(outer, shift_ref, own_ref, *refs):
    shifted = shift_ref[0]
    if outer:
        left_ref, right_ref, done_ref, q_ref, k_ref, v_ref, p_ref, att_ref, wide, win, back, flat = refs
        windows = (0, 3)
    else:
        q_ref, k_ref, v_ref, p_ref, out_ref, wide, win = refs
        windows = (1, 2)
    factor = (D // NH) ** (-0.5)
    for row in range(ROWS_DEV):
        for i in range(3):
            line = row * 3 + i
            wide[line, COLS_DEV + 2 * WIN - 3 : SPAN, :] = jnp.zeros((8, D), f32)
            wide[line, WIN : WIN + COLS_DEV, :] = own_ref[row, i].astype(f32)
            if outer:
                wide[line, :WIN, :] = left_ref[row, i].astype(f32)
                wide[line, WIN + COLS_DEV : 2 * WIN + COLS_DEV, :] = right_ref[row, i].astype(f32)
            else:
                wide[line, :WIN, :] = jnp.zeros((WIN, D), f32)
                wide[line, WIN + COLS_DEV : 2 * WIN + COLS_DEV, :] = jnp.zeros((WIN, D), f32)
            wide[line] = pltpu.roll(wide[line], SPAN - WIN + shifted, 0)
            for at_w, w in enumerate(windows):
                win[i, at_w, row * 8 : (row + 1) * 8, :] = wide[line, WIN * w : WIN * w + 8, :]
    win[:, :, KEYS - 8 :, :] = jnp.zeros((3, 2, 8, D), f32)
    masks = head_masks(bf16)
    key = iota((KEYS, LANES), 1) & (KEYS - 1)
    real = (key < ROWS_DEV * 8) & ((key & 7) < WIN)

    def window(w, carry):
        q_ref[w] = win[0, w].astype(bf16)
        k_ref[w] = win[1, w].astype(bf16)
        v_ref[w] = win[2, w].astype(bf16)
        for block in range(GROUPS):
            at = slice(block * LANES, (block + 1) * LANES)
            keys = by_head(k_ref[w, :, at], masks)
            values = by_head(v_ref[w, :, at], masks)
            scores = mm_cols(q_ref[w, :, at], keys) * factor
            parts = []
            for half in range(2):
                held = jnp.where(real, scores[:, half * LANES : (half + 1) * LANES], -1e30)
                raised = jnp.exp(held - half_max(held))
                probs = raised / half_sum(raised)
                base = (2 * block + half) * LANES
                p_ref[w, :, base : base + LANES] = probs
                parts.append(probs.astype(bf16))
            win[0, w, :, at] = mm(jnp.concatenate(parts, axis=1), values)
        return carry

    lax.fori_loop(0, 2, window, 0)
    if not outer:
        out_ref[...] = win[0].astype(bf16)
        return
    win[1] = done_ref[...].astype(f32)
    flat[...] = jnp.zeros_like(flat)
    for row in range(ROWS_DEV):
        span = slice(row * 8, (row + 1) * 8)
        back[row, 0:8, :] = win[0, 0, span, :]
        back[row, WIN : WIN + 8, :] = win[1, 0, span, :]
        back[row, 2 * WIN : 2 * WIN + 8, :] = win[1, 1, span, :]
        back[row, 3 * WIN : 3 * WIN + 8, :] = win[0, 1, span, :]
        turned = pltpu.roll(back[row], jnp.where(shifted == 0, 0, LINES - shifted), 0)
        flat[row * PITCH : row * PITCH + COLS_DEV, :] = turned[:COLS_DEV]
    att_ref[...] = flat[...].astype(bf16)


def attend(shifted, own, edges=()):
    inner = pl.BlockSpec(memory_space=pltpu.VMEM)
    last = shape((2, KEYS, D), bf16)
    scratch = [pltpu.VMEM((3 * ROWS_DEV, SPAN, D), f32), pltpu.VMEM((3, 2, KEYS, D), f32)]
    if edges:
        last = shape((PAY_ROWS, D), bf16)
        scratch += [pltpu.VMEM((ROWS_DEV, LINES, D), f32), pltpu.VMEM((PAY_ROWS, D), f32)]
    return call(
        functools.partial(attend_kernel, bool(edges)),
        56,
        (*3 * [shape((2, KEYS, D), bf16)], shape((2, KEYS, 2 * D), f32), last),
        1_000_000 if edges else 9_000_000_000,
        1_000_000 if edges else 6_000_000,
        scratch,
        in_specs=[pl.BlockSpec(memory_space=pltpu.SMEM)] + [inner] * (1 + len(edges)),
    )(shifted, own, *edges)


def attend_grad_kernel(
    outer, shift_ref, own_ref, q_ref, k_ref, v_ref, p_ref, *refs
):
    shifted = shift_ref[0]
    if outer:
        left_ref, right_ref, done_ref, out_ref, wide, win, back = refs
        win[:, 1:3] = done_ref[...].astype(f32)
        windows = (0, 3)
    else:
        out_ref, wide, win = refs
        windows = (1, 2)
    factor = (D // NH) ** (-0.5)
    valid = jnp.where(iota((8, 1), 0) < WIN, 1.0, 0.0)
    for row in range(ROWS_DEV):
        wide[row, COLS_DEV + 2 * WIN - 3 : SPAN, :] = jnp.zeros((8, D), f32)
        wide[row, WIN : WIN + COLS_DEV, :] = own_ref[row].astype(f32)
        if outer:
            wide[row, :WIN, :] = left_ref[row].astype(f32)
            wide[row, WIN + COLS_DEV : 2 * WIN + COLS_DEV, :] = right_ref[row].astype(f32)
        else:
            wide[row, :WIN, :] = jnp.zeros((WIN, D), f32)
            wide[row, WIN + COLS_DEV : 2 * WIN + COLS_DEV, :] = jnp.zeros((WIN, D), f32)
        wide[row] = pltpu.roll(wide[row], SPAN - WIN + shifted, 0)
        for w in windows:
            win[0, w, row * 8 : (row + 1) * 8, :] = wide[row, WIN * w : WIN * w + 8, :] * valid
    for w in windows:
        win[0, w, KEYS - 8 :, :] = jnp.zeros((8, D), f32)
    masks = head_masks(bf16)
    wide_masks = head_masks(f32)

    def gathered(values):
        return sum(
            wide_masks[j] * values[j * KEYS : (j + 1) * KEYS] for j in range(PER)
        )

    def window(at_w, carry):
        w = 3 * at_w if outer else at_w + 1
        for block in range(GROUPS):
            at = slice(block * LANES, (block + 1) * LANES)
            upstream = win[0, w, :, at].astype(bf16)
            keys = by_head(k_ref[at_w, :, at], masks)
            values = by_head(v_ref[at_w, :, at], masks)
            grad_probs = mm_cols(upstream, values)
            low = []
            grads = []
            for half in range(2):
                base = (2 * block + half) * LANES
                probs = p_ref[at_w, :, base : base + LANES]
                part = grad_probs[:, half * LANES : (half + 1) * LANES]
                grads.append((probs * (part - half_sum(part * probs)) * factor).astype(bf16))
                low.append(probs.astype(bf16))
            grad_scores = jnp.concatenate(grads, axis=1)
            win[0, w, :, at] = mm(grad_scores, keys)
            win[1, w, :, at] = gathered(mm_rows(grad_scores, q_ref[at_w, :, at]))
            win[2, w, :, at] = gathered(mm_rows(jnp.concatenate(low, axis=1), upstream))
        return carry

    lax.fori_loop(0, 2, window, 0)
    if not outer:
        out_ref[...] = win[:, 1:3].astype(bf16)
        return
    for row in range(ROWS_DEV):
        for i in range(3):
            line = row * 3 + i
            for w in range(4):
                back[line, WIN * w : WIN * w + 8, :] = win[i, w, row * 8 : (row + 1) * 8, :]
            turned = pltpu.roll(back[line], jnp.where(shifted == 0, 0, LINES - shifted), 0)
            out_ref[row, i] = turned[:COLS_DEV].astype(bf16)


def attend_grad(shifted, own, saved, edges=()):
    inner = pl.BlockSpec(memory_space=pltpu.VMEM)
    part = shape((3, 2, KEYS, D), bf16)
    scratch = [pltpu.VMEM((ROWS_DEV, SPAN, D), f32), pltpu.VMEM((3, 4, KEYS, D), f32)]
    if edges:
        part = shape((ROWS_DEV, 3, COLS_DEV, D), bf16)
        scratch.append(pltpu.VMEM((3 * ROWS_DEV, LINES, D), f32))
    return call(
        functools.partial(attend_grad_kernel, bool(edges)),
        56,
        part,
        10_000_000_000,
        6_000_000,
        scratch,
        in_specs=[pl.BlockSpec(memory_space=pltpu.SMEM)] + [inner] * (5 + len(edges)),
    )(shifted, own, *saved, *edges)


def halo(values, axis):
    count = lax.axis_size("lon")
    length = values.shape[axis]
    left = lax.ppermute(
        lax.slice_in_dim(values, length - WIN, length, axis=axis),
        "lon",
        [(i, (i + 1) % count) for i in range(count)],
    )
    right = lax.ppermute(
        lax.slice_in_dim(values, 0, WIN, axis=axis),
        "lon",
        [((i + 1) % count, i) for i in range(count)],
    )
    return (left, values, right)


def shards(
    resid, qkv, out_proj, norm_gain, router, w_in, w_out, expert_ids, slots, shifts, grad_out
):
    lat = lax.axis_index("lat")
    lon = lax.axis_index("lon")
    router_t = router.T
    gain = norm_gain.reshape(1, D)
    places = (expert_ids.transpose(0, 2, 1), slots.transpose(0, 2, 1))
    send, split_router, routed_in, normed, stats, back_at = front(
        resid, grad_out, gain, router_t, *places
    )
    shifted = shifts[lat].reshape(1)
    send, here = lax.optimization_barrier((send, qkv.transpose(0, 2, 1, 3)))
    got = spread(send)
    *inside, attended = attend(shifted, here)
    got, attended, here = lax.optimization_barrier((got, attended, here))
    own = unfold(got)
    own, here = lax.optimization_barrier((own, here))
    left, here, right = halo(here, 2)
    far = [swap(part, 2) for part in own]
    near = [swap(part, 1) for part in own]

    expert = lon.astype(jnp.int32).reshape(1)
    weights = (w_in[0], w_out[0], split_router)
    chunks = [*own, *near]
    dx_own, dx_near, cu, dh = experts(expert, chunks, *weights)
    cus, dhs, far_sums = ([cu], [dh], [])
    far[0], dx_own, left, right = lax.optimization_barrier((far[0], dx_own, left, right))
    near_sum = swap(dx_near, 1)
    for part in range(2):
        pair = [far[part], swap(far[part], 1)]
        if part == 1:
            *pair, pair_sum = lax.optimization_barrier((*pair, pair_sum))
            far_sums.append(swap(pair_sum, 2))
        dx_far, dx_cross, cu, dh = experts(expert, pair, *weights)
        if part == 0:
            far[1], dx_far, dx_cross = lax.optimization_barrier((far[1], dx_far, dx_cross))
            dx_cross = swap(dx_cross, 1)
        else:
            dx_cross, far_sums[0] = lax.optimization_barrier((swap(dx_cross, 1), far_sums[0]))
        pair_sum = (dx_far.astype(f32) + dx_cross.astype(f32)).astype(bf16)
        chunks += pair
        cus.append(cu)
        dhs.append(dh)
    far_sums.append(swap(pair_sum, 2))
    folded = fold(dx_own, near_sum, *far_sums)
    folded, chunks, cus, dhs, left, right = lax.optimization_barrier(
        (folded, chunks, cus, dhs, left, right)
    )
    back = spread(folded)
    *outside, attended = attend(shifted, here, (left, right, attended))
    core = lat & 1

    def side_for(core):
        return jnp.concatenate(
            [
                lax.dynamic_slice_in_dim(values, (2 * block + core) * QUARTER, QUARTER, 1)
                for values in (routed_in, attended)
                for block in range(2)
            ],
            axis=1,
        )

    sides = (side_for(core), side_for(1 - core))
    d_w_in = weight_grad([(chunk, 0) for chunk in chunks], [(dh, None) for dh in dhs])
    d_w_out = weight_grad([(cu, None) for cu in cus], [(chunk, 1) for chunk in chunks])
    back, sides, d_w_in, d_w_out = lax.optimization_barrier((back, sides, d_w_in, d_w_out))
    d_resid, d_attn, pay = middle(
        back, back_at, normed, stats, grad_out, gain, router_t, out_proj
    )
    pays = (pay, swap(pay, 1))
    shares = share(core.astype(jnp.int32).reshape(1), *pays, sides[0], swap(sides[1], 1))
    shares, d_attn = lax.optimization_barrier((shares, d_attn))
    left, d_attn, right = halo(d_attn, 1)
    middle_grads = attend_grad(shifted, d_attn, inside)
    shares = shares.reshape(2 * RING, RING * SHARE_ROWS, LANES)
    shares = exchange(shares, ("lat", "lon"), ACROSS)
    shares, middle_grads = lax.optimization_barrier((shares, middle_grads))
    shares = tally(shares).reshape(RING, SHARE_ROWS, LANES)
    left, right, shares = lax.optimization_barrier((left, right, shares))
    d_qkv = attend_grad(shifted, d_attn, outside, (left, right, middle_grads)).transpose(0, 2, 1, 3)
    proj_share, router_share, gain_share = finish(exchange(shares, groups=ALONG))
    return (
        d_resid,
        d_qkv,
        proj_share,
        gain_share.reshape(4),
        router_share,
        d_w_in[None],
        d_w_out[None],
    )


def solution(mesh):
    in_specs = (
        P("lat", "lon", None),
        P("lat", "lon", None, None),
        P(),
        P(),
        P(),
        P("lon", None, "lat"),
        P("lon", "lat", None),
        P("lat", "lon", None),
        P("lat", "lon", None),
        P(),
        P("lat", "lon", None),
    )
    out_specs = (
        P("lat", "lon", None),
        P("lat", "lon", None, None),
        P(("lat", "lon"), None),
        P(("lat", "lon")),
        P(("lat", "lon"), None),
        P("lon", None, "lat"),
        P("lon", "lat", None),
    )
    return jax.shard_map(shards, mesh=mesh, in_specs=in_specs, out_specs=out_specs, check_vma=False)
```

```python
import functools

import jax
import jax.numpy as jnp
from jax import lax
from jax.experimental import pallas as pl
from jax.experimental.pallas import tpu as pltpu
from jax.sharding import PartitionSpec as P

D = 1024
NH = 32
WIN = 7
ROWS_DEV = 7
COLS_DEV = 21
PITCH = 24
TOK = ROWS_DEV * PITCH
EXPERTS = 64
CAP = 5
LANES = 128
BLOCKS = D // LANES
SLOTS = EXPERTS * CAP
SEND_ROWS = 2 * CAP * BLOCKS
BACK_ROWS = CAP * BLOCKS + 8
SHARE_ROWS = 40
PAY_ROWS = TOK + 8
WIDE = D + LANES

norm_eps = 1e-05
zloss_weight = 0.25
bf16 = jnp.bfloat16
f32 = jnp.float32
MEBI = 1024 * 1024


def call(kernel, vmem, out_shape, flops, moved, scratch=(), **kwargs):
    return pl.pallas_call(
        kernel,
        out_shape=out_shape,
        scratch_shapes=list(scratch),
        compiler_params=pltpu.CompilerParams(vmem_limit_bytes=vmem * MEBI),
        cost_estimate=pl.CostEstimate(flops=flops, bytes_accessed=moved, transcendentals=0),
        **kwargs,
    )


def mm(left, right):
    return lax.dot_general(left, right, (((1,), (0,)), ((), ())), preferred_element_type=f32)


def mm_cols(left, right):
    return lax.dot_general(left, right, (((1,), (1,)), ((), ())), preferred_element_type=f32)


def mm_rows(left, right):
    return lax.dot_general(left, right, (((0,), (0,)), ((), ())), preferred_element_type=f32)


def shape(dims, kind):
    return jax.ShapeDtypeStruct(dims, kind)


def iota(dims, axis):
    return lax.broadcasted_iota(jnp.int32, dims, axis)


def split3(value):
    high = value.astype(bf16)
    rest = value - high.astype(f32)
    middle = rest.astype(bf16)
    return (high, middle, (rest - middle.astype(f32)).astype(bf16))


def softmax_parts(logits):
    held = jnp.where(iota(logits.shape, 1) < EXPERTS, logits, -1e30)
    top = jnp.max(held, axis=-1, keepdims=True)
    raised = jnp.exp(held - top)
    total = jnp.sum(raised, axis=-1, keepdims=True)
    return (raised / total, top + jnp.log(total))


def three_logits(rows, split_router):
    triple = mm_cols(rows, split_router)
    return triple[:, 2 * LANES :] + triple[:, LANES : 2 * LANES] + triple[:, :LANES]


def front_kernel(
    resid_ref, grad_ref, gain_ref, router_ref, ids_ref, slots_ref,
    send_ref, split_ref, z_ref, normed_ref, stats_ref, back_ref, rows, folded, target_ref,
):
    target_ref[...] = jnp.full((2, 2 * TOK), -1, jnp.int32)
    back_ref[...] = jnp.full((2, TOK), -1, jnp.int32)
    for row in range(ROWS_DEV):
        ids = ids_ref[row]
        spots = slots_ref[row]
        base = row * PITCH
        back_ref[:, base : base + COLS_DEV] = spots * EXPERTS + ids
        target_ref[:, base : base + COLS_DEV] = ids * (2 * CAP) + spots
        target_ref[:, TOK + base : TOK + base + COLS_DEV] = ids * (2 * CAP) + spots + CAP
    rows[...] = jnp.zeros_like(rows)
    for row in range(ROWS_DEV):
        rows[row * PITCH : row * PITCH + COLS_DEV, :] = resid_ref[row].astype(f32)
        base = TOK + row * PITCH
        rows[base : base + COLS_DEV, :] = grad_ref[row].astype(f32)
    resid = rows[:TOK, :]
    center = resid - jnp.mean(resid, axis=-1, keepdims=True)
    inv_std = lax.rsqrt(jnp.mean(center * center, axis=-1, keepdims=True) + norm_eps)
    normed = center * inv_std
    normed_ref[...] = normed
    rows[:TOK, :] = normed * gain_ref[...]
    both = rows[...].astype(bf16)
    slot = iota((2 * SLOTS, 2 * TOK), 0)
    pick = jnp.where(
        (slot == target_ref[0:1, :]) | (slot == target_ref[1:2, :]), 1.0, 0.0
    ).astype(bf16)
    for pair in range(BLOCKS // 2):
        got = mm(pick, both[:, pair * 2 * LANES : (pair + 1) * 2 * LANES])
        for half in range(2):
            folded[pl.ds(2 * pair + half, 2 * SLOTS, stride=BLOCKS), :] = got[
                :, half * LANES : (half + 1) * LANES
            ]
    send_ref[...] = folded[...].astype(bf16)
    empty = jnp.zeros((LANES - EXPERTS, D), bf16)
    for index, part in enumerate(split3(router_ref[...])):
        split_ref[index * LANES : index * LANES + EXPERTS, :] = part
        split_ref[index * LANES + EXPERTS : (index + 1) * LANES, :] = empty
    z_ref[...] = jnp.where(iota((PAY_ROWS, 1), 0) < TOK, rows[:PAY_ROWS, :], 0.0).astype(bf16)
    probs, log_total = softmax_parts(three_logits(both[:PAY_ROWS, :], split_ref[...]))
    stats_ref[:, :LANES] = probs[:TOK]
    stats_ref[:, LANES : 2 * LANES] = jnp.broadcast_to(log_total[:TOK], (TOK, LANES))
    stats_ref[:, 2 * LANES :] = jnp.broadcast_to(inv_std, (TOK, LANES))


def front(resid, grad, gain, router_t, ids, slots):
    return call(
        front_kernel,
        56,
        (
            shape((EXPERTS * SEND_ROWS, LANES), bf16),
            shape((3 * LANES, D), bf16),
            shape((PAY_ROWS, D), bf16),
            shape((TOK, D), f32),
            shape((TOK, 3 * LANES), f32),
            shape((2, TOK), jnp.int32),
        ),
        4_600_000_000,
        4_000_000,
        [
            pltpu.VMEM((2 * TOK, D), f32),
            pltpu.VMEM((EXPERTS * SEND_ROWS, LANES), f32),
            pltpu.VMEM((2, 2 * TOK), jnp.int32),
        ],
    )(resid, grad, gain, router_t, ids, slots)


PARTS = (3 * EXPERTS, 2 * EXPERTS)


def unfold_kernel(got_ref, first_ref, second_ref, wide):
    wide[...] = got_ref[...].astype(f32)
    for c in range(2 * CAP):
        ref, place = (first_ref, c % CAP) if c % CAP < 3 else (second_ref, c % CAP - 3)
        base = place * EXPERTS + (c // CAP) * ref.shape[0] // 2
        for s in range(BLOCKS):
            ref[base : base + EXPERTS, s * LANES : (s + 1) * LANES] = wide[
                pl.ds(c * BLOCKS + s, EXPERTS, stride=SEND_ROWS), :
            ].astype(bf16)


def unfold(got):
    return call(
        unfold_kernel,
        14,
        tuple(shape((2 * part, D), bf16) for part in PARTS),
        3_900_000_000,
        2_600_000,
        [pltpu.VMEM((EXPERTS * SEND_ROWS, LANES), f32)],
    )(got)


FF_TILE = 256


def expert_kernel(count, expert_ref, *refs):
    chunks = refs[:count]
    in_ref, out_w_ref, split_ref, near_ref, far_ref, cu_ref, dh_ref = refs[count : count + 7]
    inputs, grads, total, dc, comb = refs[count + 7 :]
    step = pl.program_id(0)
    rows = inputs.shape[0]

    @pl.when(step == 0)
    def _():
        base = 0
        for ref in chunks:
            part = ref.shape[0] // 2
            inputs[base : base + part, :] = ref[:part, :]
            grads[base : base + part, :] = ref[part:, :]
            base += part
        probs, _unused = softmax_parts(three_logits(inputs[...], split_ref[...]))
        mine = jnp.where(iota(probs.shape, 1) == expert_ref[0], probs, 0.0)
        weight = jnp.sum(mine, axis=-1, keepdims=True).astype(bf16).astype(f32)
        comb[...] = jnp.broadcast_to(weight, (rows, LANES))
        dc[...] = jnp.zeros_like(dc)
        total[...] = jnp.zeros_like(total)

    weight_in = in_ref[...]
    hidden = mm(inputs[...], weight_in)
    grad_w = mm_cols(grads[...], out_w_ref[...])
    cdf = 0.5 * (1.0 + lax.erf(hidden * 0.7071067811865476))
    active = hidden * cdf
    slope = cdf + hidden * jnp.exp(-0.5 * hidden * hidden) * 0.3989422804014327
    dc[...] += jnp.broadcast_to(jnp.sum(active * grad_w, axis=-1, keepdims=True), (rows, LANES))
    weight = comb[:, 0:1]
    cu_ref[...] = (weight * active).astype(bf16)
    grad_hidden = (weight * grad_w * slope).astype(bf16)
    dh_ref[...] = grad_hidden
    total[...] += mm_cols(grad_hidden, weight_in)

    @pl.when(step == pl.num_programs(0) - 1)
    def _():
        for index, ref in enumerate((near_ref, far_ref)):
            span = slice(index * rows // 2, (index + 1) * rows // 2)
            ref[:, :D] = total[span, :].astype(bf16)
            ref[:, D:] = dc[span, :].astype(bf16)


def experts(expert, chunks, weight_in, weight_out, split_router):
    width = weight_in.shape[1]
    count = len(chunks)
    rows = sum(chunk.shape[0] for chunk in chunks) // 2
    whole = lambda dims: pl.BlockSpec(dims, lambda j: (0,) * len(dims))
    return call(
        functools.partial(expert_kernel, count),
        56 if count == 4 else 30,
        (
            shape((rows // 2, WIDE), bf16),
            shape((rows // 2, WIDE), bf16),
            shape((rows, width), bf16),
            shape((rows, width), bf16),
        ),
        22 * rows * D * width,
        12_000_000,
        [
            pltpu.VMEM((rows, D), bf16),
            pltpu.VMEM((rows, D), bf16),
            pltpu.VMEM((rows, D), f32),
            pltpu.VMEM((rows, LANES), f32),
            pltpu.VMEM((rows, LANES), f32),
        ],
        grid=(width // FF_TILE,),
        in_specs=[pl.BlockSpec(memory_space=pltpu.SMEM)]
        + [whole(chunk.shape) for chunk in chunks]
        + [
            pl.BlockSpec((D, FF_TILE), lambda j: (0, j)),
            pl.BlockSpec((FF_TILE, D), lambda j: (j, 0)),
            whole((3 * LANES, D)),
        ],
        out_specs=(
            whole((rows // 2, WIDE)),
            whole((rows // 2, WIDE)),
            pl.BlockSpec((rows, FF_TILE), lambda j: (0, j)),
            pl.BlockSpec((rows, FF_TILE), lambda j: (0, j)),
        ),
    )(expert, *chunks, weight_in, weight_out, split_router)


def weight_kernel(count, *refs):
    left, right, (out_ref, left_rows, right_rows) = (refs[:count], refs[count:-3], refs[-3:])

    def gather(parts, stack):
        base = 0
        for ref in parts:
            stack[base : base + ref.shape[0], :] = ref[...]
            base += ref.shape[0]

    @pl.when(pl.program_id(0) == 0)
    def _():
        gather(right, right_rows)

    gather(left, left_rows)
    out_ref[...] = mm_rows(left_rows[...], right_rows[...]).astype(bf16)


def weight_grad(left, right):
    block = 256

    def rows(pair):
        return pair[0].shape[0] // (1 if pair[1] is None else 2)

    def spec(pair, wide):
        half = pair[1] or 0
        if wide:
            return pl.BlockSpec((rows(pair), D), lambda j: (half, 0))
        return pl.BlockSpec((rows(pair), block), lambda j: (half, j))

    total = sum(rows(pair) for pair in left)
    return call(
        functools.partial(weight_kernel, len(left)),
        56,
        shape((D, D), bf16),
        1_000_000,
        1_000_000,
        [pltpu.VMEM((total, block), bf16), pltpu.VMEM((total, D), bf16)],
        grid=(D // block,),
        in_specs=[spec(pair, False) for pair in left] + [spec(pair, True) for pair in right],
        out_specs=pl.BlockSpec((block, D), lambda j: (j, 0)),
    )(*[pair[0] for pair in left], *[pair[0] for pair in right])


def fold_kernel(own_ref, near_ref, first_ref, second_ref, out_ref, folded, total):
    total[...] = own_ref[...].astype(f32) + near_ref[...].astype(f32)
    total[: PARTS[0], :] += first_ref[...].astype(f32)
    total[PARTS[0] :, :] += second_ref[...].astype(f32)
    for c in range(CAP):
        part = total[c * EXPERTS : (c + 1) * EXPERTS, :]
        for s in range(BLOCKS):
            folded[pl.ds(c * BLOCKS + s, EXPERTS, stride=BACK_ROWS), :] = part[
                :, s * LANES : (s + 1) * LANES
            ]
        folded[pl.ds(CAP * BLOCKS + c, EXPERTS, stride=BACK_ROWS), :] = part[:, D:]
    for spare in range(CAP * BLOCKS + CAP, BACK_ROWS):
        folded[pl.ds(spare, EXPERTS, stride=BACK_ROWS), :] = jnp.zeros((EXPERTS, LANES), f32)
    out_ref[...] = folded[...].astype(bf16)


def fold(own, near, first, second):
    return call(
        fold_kernel,
        14,
        shape((EXPERTS * BACK_ROWS, LANES), bf16),
        3_800_000_000,
        3_000_000,
        [pltpu.VMEM((EXPERTS * BACK_ROWS, LANES), f32), pltpu.VMEM((SLOTS, WIDE), f32)],
    )(own, near, first, second)


def middle_kernel(
    back_ref, target_ref, normed_ref, stats_ref, grad_ref, gain_ref, router_ref, proj_ref,
    resid_ref, attn_ref, pay_ref, wide, table, rows,
):
    wide[...] = back_ref[...].astype(f32)
    lane = iota((EXPERTS, LANES), 1)
    same = lane == iota((EXPERTS, LANES), 0)
    for c in range(CAP):
        span = slice(c * EXPERTS, (c + 1) * EXPERTS)
        for s in range(BLOCKS):
            table[span, s * LANES : (s + 1) * LANES] = wide[
                pl.ds(c * BLOCKS + s, EXPERTS, stride=BACK_ROWS), :
            ].astype(bf16)
        weights = wide[pl.ds(CAP * BLOCKS + c, EXPERTS, stride=BACK_ROWS), :]
        table[span, D:] = jnp.where(same, weights, 0.0).astype(bf16)
    slot = iota((SLOTS, TOK), 0)
    pick = jnp.where(
        (slot == target_ref[0:1, :]) | (slot == target_ref[1:2, :]), 1.0, 0.0
    ).astype(bf16)
    routed = mm_rows(pick, table[...])
    grad_probs = routed[:, D:]
    probs = stats_ref[:, :LANES]
    log_total = stats_ref[:, LANES : 2 * LANES]
    inv_std = stats_ref[:, 2 * LANES : 2 * LANES + 1]
    grad_logits = (
        probs * (grad_probs - jnp.sum(probs * grad_probs, axis=-1, keepdims=True))
        + 2.0 * zloss_weight * log_total * probs
    )
    grad_z = routed[:, :D] + jnp.dot(
        grad_logits[:, :EXPERTS], router_ref[...], precision=lax.Precision.HIGHEST,
        preferred_element_type=f32,
    )
    normed = normed_ref[...]
    gain_term = jnp.sum(grad_z * normed, axis=0, keepdims=True)
    rows[...] = jnp.zeros_like(rows)
    for row in range(ROWS_DEV):
        rows[row * PITCH : row * PITCH + COLS_DEV, :] = grad_ref[row].astype(f32)
    grad_normed = grad_z * gain_ref[...]
    rows[:TOK, :] = rows[:TOK, :] + inv_std * (
        grad_normed
        - jnp.mean(grad_normed, axis=-1, keepdims=True)
        - normed * jnp.mean(grad_normed * normed, axis=-1, keepdims=True)
    )
    for row in range(ROWS_DEV):
        resid_ref[row] = rows[row * PITCH : row * PITCH + COLS_DEV, :].astype(bf16)
    low = rows[...].astype(bf16)
    rows[...] = mm_cols(low, proj_ref[...])
    for row in range(ROWS_DEV):
        attn_ref[row] = rows[row * PITCH : row * PITCH + COLS_DEV, :].astype(bf16)
    high, middle, last = (part.astype(f32) for part in split3(gain_term))
    extra = iota((PAY_ROWS, 1), 0)
    rows[...] = jnp.where(
        extra < TOK,
        low.astype(f32),
        jnp.where(
            extra == TOK, high, jnp.where(extra == TOK + 1, middle, jnp.where(extra == TOK + 2, last, 0.0))
        ),
    )
    pay_ref[:, :D] = rows[...].astype(bf16)
    upper = grad_logits.astype(bf16).astype(f32)
    lower = (grad_logits - upper).astype(bf16).astype(f32)
    mixed = upper + pltpu.roll(lower, EXPERTS, 1)
    pay_ref[:, D:] = jnp.concatenate([mixed, jnp.zeros((PAY_ROWS - TOK, LANES), f32)], axis=0).astype(bf16)


def middle(back, targets, normed, stats, grad, gain, router_t, out_proj):
    return call(
        middle_kernel,
        56,
        (
            shape((ROWS_DEV, COLS_DEV, D), bf16),
            shape((ROWS_DEV, COLS_DEV, D), bf16),
            shape((PAY_ROWS, WIDE), bf16),
        ),
        7_000_000_000,
        6_000_000,
        [
            pltpu.VMEM((EXPERTS * BACK_ROWS, LANES), f32),
            pltpu.VMEM((SLOTS, WIDE), bf16),
            pltpu.VMEM((PAY_ROWS, D), f32),
        ],
    )(back, targets, normed, stats, grad, gain, router_t, out_proj)


SHARED = EXPERTS * SHARE_ROWS
QUARTER = D // 4


def share_kernel(core_ref, pay_ref, pay_near_ref, side_ref, side_near_ref, out_ref, folded):
    both = ((pay_ref, side_ref), (pay_near_ref, side_near_ref))
    gain = jnp.zeros((1, D), f32)
    at = iota((16, 1), 0)
    for pay, _unused in both:
        last = pay[PAY_ROWS - 16 :, :D].astype(f32)
        gain += jnp.sum(jnp.where((at >= 8) & (at < 11), last, 0.0), axis=0, keepdims=True)
    same = iota((QUARTER, QUARTER), 0) == iota((QUARTER, QUARTER), 1)
    lane = iota((QUARTER, LANES), 1)
    step = SHARE_ROWS // 4
    for block in range(2):
        z_at = slice(block * QUARTER, (block + 1) * QUARTER)
        a_at = slice((2 + block) * QUARTER, (3 + block) * QUARTER)
        proj = sum(mm_rows(side[:, a_at], pay[:, :D]) for pay, side in both)
        router = sum(mm_rows(side[:, z_at], pay[:, D:]) for pay, side in both)
        mine = jnp.zeros((1, QUARTER), f32)
        for core in range(2):
            place = (2 * block + core) * QUARTER
            mine += jnp.where(core_ref[0] == core, gain[:, place : place + QUARTER], 0.0)
        column = jnp.sum(jnp.where(same, mine, 0.0), axis=-1, keepdims=True)
        router = router + pltpu.roll(router, EXPERTS, 1)
        extra = jnp.where(lane < EXPERTS, router, jnp.where(lane == EXPERTS, column, 0.0))
        upper = extra.astype(bf16).astype(f32)
        base = block * SHARED
        for s in range(BLOCKS):
            folded[pl.ds(base + s, QUARTER, stride=step), :] = proj[:, s * LANES : (s + 1) * LANES]
        folded[pl.ds(base + BLOCKS, QUARTER, stride=step), :] = upper
        folded[pl.ds(base + BLOCKS + 1, QUARTER, stride=step), :] = extra - upper
    out_ref[...] = folded[...].astype(bf16)


def share(core, *arrays):
    inner = pl.BlockSpec(memory_space=pltpu.VMEM)
    return call(
        share_kernel,
        20,
        shape((2 * SHARED, LANES), bf16),
        3_900_000_000,
        4_000_000,
        [pltpu.VMEM((2 * SHARED, LANES), f32)],
        in_specs=[pl.BlockSpec(memory_space=pltpu.SMEM)] + [inner] * 4,
    )(core, *arrays)


def tally_kernel(got_ref, out_ref):
    out_ref[...] = sum(got_ref[k].astype(f32) for k in range(got_ref.shape[0]))


def tally(got):
    return call(tally_kernel, 8, shape(got.shape[1:], f32), 1_000_000_000, 1_500_000)(got)


def finish_kernel(got_ref, proj_ref, router_ref, gain_ref):
    total = sum(got_ref[k] for k in range(got_ref.shape[0]))
    step = SHARE_ROWS // 4
    lane = iota((1, 4), 1)
    gain = jnp.zeros((1, 4), f32)
    for r in range(4):
        for s in range(BLOCKS):
            proj_ref[r : r + 1, s * LANES : (s + 1) * LANES] = total[r * step + s : r * step + s + 1]
        at = r * step + BLOCKS
        extra = total[at : at + 1] + total[at + 1 : at + 2]
        router_ref[r : r + 1, :] = extra[:, :EXPERTS]
        gain = jnp.where(lane == r, extra[:, EXPERTS : EXPERTS + 1], gain)
    gain_ref[...] = gain


def finish(got):
    return call(
        finish_kernel,
        4,
        (shape((4, D), f32), shape((4, EXPERTS), f32), shape((1, 4), f32)),
        1_000_000_000,
        200_000,
    )(got)


def swap(value, step):
    return lax.ppermute(value, "lat", [(k, k ^ step) for k in range(4)])


def exchange(value, axes="lon", groups=None):
    return lax.all_to_all(
        value, axes, split_axis=0, concat_axis=0, tiled=True, axis_index_groups=groups
    )


def spread(value):
    return exchange(value.reshape(EXPERTS, -1, LANES)).reshape(-1, LANES)


RING = 8
ALONG = [[line * RING + k for k in range(RING)] for line in range(EXPERTS // RING)]
ACROSS = [
    [
        (2 * row + core) * EXPERTS + line * RING + k
        for row in range(2)
        for line in range(EXPERTS // RING)
    ]
    for core in range(2)
    for k in range(RING)
]


KEYS = 64
GROUPS = D // LANES
PER = LANES // (D // NH)
SPAN = 40
LINES = 32


def head_masks(kind):
    lane = iota((KEYS, LANES), 1) // (D // NH)
    return [jnp.where(lane == j, 1.0, 0.0).astype(kind) for j in range(PER)]


def by_head(values, masks):
    return jnp.concatenate([values * mask for mask in masks], axis=0)


def halves(values, pick):
    first = iota(values.shape, 1) < KEYS
    left = pick(values, first)
    right = pick(values, jnp.logical_not(first))
    return jnp.where(first, left, right)


def half_sum(values):
    return halves(
        values, lambda v, m: jnp.sum(jnp.where(m, v, 0.0), axis=-1, keepdims=True)
    )


def half_max(values):
    return halves(
        values, lambda v, m: jnp.max(jnp.where(m, v, -3e38), axis=-1, keepdims=True)
    )


def attend_kernel(outer, shift_ref, own_ref, *refs):
    shifted = shift_ref[0]
    if outer:
        left_ref, right_ref, done_ref, q_ref, k_ref, v_ref, p_ref, att_ref, wide, win, back, flat = refs
        windows = (0, 3)
    else:
        q_ref, k_ref, v_ref, p_ref, out_ref, wide, win = refs
        windows = (1, 2)
    factor = (D // NH) ** (-0.5)
    for row in range(ROWS_DEV):
        for i in range(3):
            line = row * 3 + i
            wide[line, COLS_DEV + 2 * WIN - 3 : SPAN, :] = jnp.zeros((8, D), f32)
            wide[line, WIN : WIN + COLS_DEV, :] = own_ref[row, i].astype(f32)
            if outer:
                wide[line, :WIN, :] = left_ref[row, i].astype(f32)
                wide[line, WIN + COLS_DEV : 2 * WIN + COLS_DEV, :] = right_ref[row, i].astype(f32)
            else:
                wide[line, :WIN, :] = jnp.zeros((WIN, D), f32)
                wide[line, WIN + COLS_DEV : 2 * WIN + COLS_DEV, :] = jnp.zeros((WIN, D), f32)
            wide[line] = pltpu.roll(wide[line], SPAN - WIN + shifted, 0)
            for at_w, w in enumerate(windows):
                win[i, at_w, row * 8 : (row + 1) * 8, :] = wide[line, WIN * w : WIN * w + 8, :]
    win[:, :, KEYS - 8 :, :] = jnp.zeros((3, 2, 8, D), f32)
    masks = head_masks(bf16)
    key = iota((KEYS, LANES), 1) & (KEYS - 1)
    real = (key < ROWS_DEV * 8) & ((key & 7) < WIN)

    def window(w, carry):
        q_ref[w] = win[0, w].astype(bf16)
        k_ref[w] = win[1, w].astype(bf16)
        v_ref[w] = win[2, w].astype(bf16)
        for block in range(GROUPS):
            at = slice(block * LANES, (block + 1) * LANES)
            keys = by_head(k_ref[w, :, at], masks)
            values = by_head(v_ref[w, :, at], masks)
            scores = mm_cols(q_ref[w, :, at], keys) * factor
            parts = []
            for half in range(2):
                held = jnp.where(real, scores[:, half * LANES : (half + 1) * LANES], -1e30)
                raised = jnp.exp(held - half_max(held))
                probs = raised / half_sum(raised)
                base = (2 * block + half) * LANES
                p_ref[w, :, base : base + LANES] = probs
                parts.append(probs.astype(bf16))
            win[0, w, :, at] = mm(jnp.concatenate(parts, axis=1), values)
        return carry

    lax.fori_loop(0, 2, window, 0)
    if not outer:
        out_ref[...] = win[0].astype(bf16)
        return
    win[1] = done_ref[...].astype(f32)
    flat[...] = jnp.zeros_like(flat)
    for row in range(ROWS_DEV):
        span = slice(row * 8, (row + 1) * 8)
        back[row, 0:8, :] = win[0, 0, span, :]
        back[row, WIN : WIN + 8, :] = win[1, 0, span, :]
        back[row, 2 * WIN : 2 * WIN + 8, :] = win[1, 1, span, :]
        back[row, 3 * WIN : 3 * WIN + 8, :] = win[0, 1, span, :]
        turned = pltpu.roll(back[row], jnp.where(shifted == 0, 0, LINES - shifted), 0)
        flat[row * PITCH : row * PITCH + COLS_DEV, :] = turned[:COLS_DEV]
    att_ref[...] = flat[...].astype(bf16)


def attend(shifted, own, edges=()):
    inner = pl.BlockSpec(memory_space=pltpu.VMEM)
    last = shape((2, KEYS, D), bf16)
    scratch = [pltpu.VMEM((3 * ROWS_DEV, SPAN, D), f32), pltpu.VMEM((3, 2, KEYS, D), f32)]
    if edges:
        last = shape((PAY_ROWS, D), bf16)
        scratch += [pltpu.VMEM((ROWS_DEV, LINES, D), f32), pltpu.VMEM((PAY_ROWS, D), f32)]
    return call(
        functools.partial(attend_kernel, bool(edges)),
        56,
        (*3 * [shape((2, KEYS, D), bf16)], shape((2, KEYS, 2 * D), f32), last),
        1_000_000 if edges else 9_000_000_000,
        1_000_000 if edges else 6_000_000,
        scratch,
        in_specs=[pl.BlockSpec(memory_space=pltpu.SMEM)] + [inner] * (1 + len(edges)),
    )(shifted, own, *edges)


def attend_grad_kernel(
    outer, shift_ref, own_ref, q_ref, k_ref, v_ref, p_ref, *refs
):
    shifted = shift_ref[0]
    if outer:
        left_ref, right_ref, done_ref, out_ref, wide, win, back = refs
        win[:, 1:3] = done_ref[...].astype(f32)
        windows = (0, 3)
    else:
        out_ref, wide, win = refs
        windows = (1, 2)
    factor = (D // NH) ** (-0.5)
    valid = jnp.where(iota((8, 1), 0) < WIN, 1.0, 0.0)
    for row in range(ROWS_DEV):
        wide[row, COLS_DEV + 2 * WIN - 3 : SPAN, :] = jnp.zeros((8, D), f32)
        wide[row, WIN : WIN + COLS_DEV, :] = own_ref[row].astype(f32)
        if outer:
            wide[row, :WIN, :] = left_ref[row].astype(f32)
            wide[row, WIN + COLS_DEV : 2 * WIN + COLS_DEV, :] = right_ref[row].astype(f32)
        else:
            wide[row, :WIN, :] = jnp.zeros((WIN, D), f32)
            wide[row, WIN + COLS_DEV : 2 * WIN + COLS_DEV, :] = jnp.zeros((WIN, D), f32)
        wide[row] = pltpu.roll(wide[row], SPAN - WIN + shifted, 0)
        for w in windows:
            win[0, w, row * 8 : (row + 1) * 8, :] = wide[row, WIN * w : WIN * w + 8, :] * valid
    for w in windows:
        win[0, w, KEYS - 8 :, :] = jnp.zeros((8, D), f32)
    masks = head_masks(bf16)
    wide_masks = head_masks(f32)

    def gathered(values):
        return sum(
            wide_masks[j] * values[j * KEYS : (j + 1) * KEYS] for j in range(PER)
        )

    def window(at_w, carry):
        w = 3 * at_w if outer else at_w + 1
        for block in range(GROUPS):
            at = slice(block * LANES, (block + 1) * LANES)
            upstream = win[0, w, :, at].astype(bf16)
            keys = by_head(k_ref[at_w, :, at], masks)
            values = by_head(v_ref[at_w, :, at], masks)
            grad_probs = mm_cols(upstream, values)
            low = []
            grads = []
            for half in range(2):
                base = (2 * block + half) * LANES
                probs = p_ref[at_w, :, base : base + LANES]
                part = grad_probs[:, half * LANES : (half + 1) * LANES]
                grads.append((probs * (part - half_sum(part * probs)) * factor).astype(bf16))
                low.append(probs.astype(bf16))
            grad_scores = jnp.concatenate(grads, axis=1)
            win[0, w, :, at] = mm(grad_scores, keys)
            win[1, w, :, at] = gathered(mm_rows(grad_scores, q_ref[at_w, :, at]))
            win[2, w, :, at] = gathered(mm_rows(jnp.concatenate(low, axis=1), upstream))
        return carry

    lax.fori_loop(0, 2, window, 0)
    if not outer:
        out_ref[...] = win[:, 1:3].astype(bf16)
        return
    for row in range(ROWS_DEV):
        for i in range(3):
            line = row * 3 + i
            for w in range(4):
                back[line, WIN * w : WIN * w + 8, :] = win[i, w, row * 8 : (row + 1) * 8, :]
            turned = pltpu.roll(back[line], jnp.where(shifted == 0, 0, LINES - shifted), 0)
            out_ref[row, i] = turned[:COLS_DEV].astype(bf16)


def attend_grad(shifted, own, saved, edges=()):
    inner = pl.BlockSpec(memory_space=pltpu.VMEM)
    part = shape((3, 2, KEYS, D), bf16)
    scratch = [pltpu.VMEM((ROWS_DEV, SPAN, D), f32), pltpu.VMEM((3, 4, KEYS, D), f32)]
    if edges:
        part = shape((ROWS_DEV, 3, COLS_DEV, D), bf16)
        scratch.append(pltpu.VMEM((3 * ROWS_DEV, LINES, D), f32))
    return call(
        functools.partial(attend_grad_kernel, bool(edges)),
        56,
        part,
        10_000_000_000,
        6_000_000,
        scratch,
        in_specs=[pl.BlockSpec(memory_space=pltpu.SMEM)] + [inner] * (5 + len(edges)),
    )(shifted, own, *saved, *edges)


def halo(values, axis):
    count = lax.axis_size("lon")
    length = values.shape[axis]
    left = lax.ppermute(
        lax.slice_in_dim(values, length - WIN, length, axis=axis),
        "lon",
        [(i, (i + 1) % count) for i in range(count)],
    )
    right = lax.ppermute(
        lax.slice_in_dim(values, 0, WIN, axis=axis),
        "lon",
        [((i + 1) % count, i) for i in range(count)],
    )
    return (left, values, right)


def shards(
    resid, qkv, out_proj, norm_gain, router, w_in, w_out, expert_ids, slots, shifts, grad_out
):
    lat = lax.axis_index("lat")
    lon = lax.axis_index("lon")
    router_t = router.T
    gain = norm_gain.reshape(1, D)
    places = (expert_ids.transpose(0, 2, 1), slots.transpose(0, 2, 1))
    send, split_router, routed_in, normed, stats, back_at = front(
        resid, grad_out, gain, router_t, *places
    )
    shifted = shifts[lat].reshape(1)
    send, here = lax.optimization_barrier((send, qkv.transpose(0, 2, 1, 3)))
    got = spread(send)
    *inside, attended = attend(shifted, here)
    got, attended, here = lax.optimization_barrier((got, attended, here))
    own = unfold(got)
    far = [swap(part, 2) for part in own]
    near = [swap(part, 1) for part in own]

    expert = lon.astype(jnp.int32).reshape(1)
    weights = (w_in[0], w_out[0], split_router)
    chunks = [*own, *near]
    dx_own, dx_near, cu, dh = experts(expert, chunks, *weights)
    cus, dhs, far_sums = ([cu], [dh], [])
    far[0], dx_own = lax.optimization_barrier((far[0], dx_own))
    near_sum = swap(dx_near, 1)
    for part in range(2):
        pair = [far[part], swap(far[part], 1)]
        if part == 1:
            *pair, pair_sum = lax.optimization_barrier((*pair, pair_sum))
            far_sums.append(swap(pair_sum, 2))
        dx_far, dx_cross, cu, dh = experts(expert, pair, *weights)
        if part == 0:
            far[1], dx_far, dx_cross = lax.optimization_barrier((far[1], dx_far, dx_cross))
            dx_cross = swap(dx_cross, 1)
        else:
            dx_cross, far_sums[0] = lax.optimization_barrier((swap(dx_cross, 1), far_sums[0]))
        pair_sum = (dx_far.astype(f32) + dx_cross.astype(f32)).astype(bf16)
        chunks += pair
        cus.append(cu)
        dhs.append(dh)
    pair_sum, here = lax.optimization_barrier((pair_sum, here))
    left, here, right = halo(here, 2)
    far_sums.append(swap(pair_sum, 2))
    folded = fold(dx_own, near_sum, *far_sums)
    folded, chunks, cus, dhs, left, right = lax.optimization_barrier(
        (folded, chunks, cus, dhs, left, right)
    )
    back = spread(folded)
    *outside, attended = attend(shifted, here, (left, right, attended))
    core = lat & 1

    def side_for(core):
        return jnp.concatenate(
            [
                lax.dynamic_slice_in_dim(values, (2 * block + core) * QUARTER, QUARTER, 1)
                for values in (routed_in, attended)
                for block in range(2)
            ],
            axis=1,
        )

    sides = (side_for(core), side_for(1 - core))
    d_w_in = weight_grad([(chunk, 0) for chunk in chunks], [(dh, None) for dh in dhs])
    d_w_out = weight_grad([(cu, None) for cu in cus], [(chunk, 1) for chunk in chunks])
    back, sides, d_w_in, d_w_out = lax.optimization_barrier((back, sides, d_w_in, d_w_out))
    d_resid, d_attn, pay = middle(
        back, back_at, normed, stats, grad_out, gain, router_t, out_proj
    )
    pays = (pay, swap(pay, 1))
    shares = share(core.astype(jnp.int32).reshape(1), *pays, sides[0], swap(sides[1], 1))
    shares, d_attn = lax.optimization_barrier((shares, d_attn))
    left, d_attn, right = halo(d_attn, 1)
    middle_grads = attend_grad(shifted, d_attn, inside)
    shares = shares.reshape(2 * RING, RING * SHARE_ROWS, LANES)
    shares = exchange(shares, ("lat", "lon"), ACROSS)
    shares, middle_grads = lax.optimization_barrier((shares, middle_grads))
    shares = tally(shares).reshape(RING, SHARE_ROWS, LANES)
    left, right, shares = lax.optimization_barrier((left, right, shares))
    d_qkv = attend_grad(shifted, d_attn, outside, (left, right, middle_grads)).transpose(0, 2, 1, 3)
    proj_share, router_share, gain_share = finish(exchange(shares, groups=ALONG))
    return (
        d_resid,
        d_qkv,
        proj_share,
        gain_share.reshape(4),
        router_share,
        d_w_in[None],
        d_w_out[None],
    )


def solution(mesh):
    in_specs = (
        P("lat", "lon", None),
        P("lat", "lon", None, None),
        P(),
        P(),
        P(),
        P("lon", None, "lat"),
        P("lon", "lat", None),
        P("lat", "lon", None),
        P("lat", "lon", None),
        P(),
        P("lat", "lon", None),
    )
    out_specs = (
        P("lat", "lon", None),
        P("lat", "lon", None, None),
        P(("lat", "lon"), None),
        P(("lat", "lon")),
        P(("lat", "lon"), None),
        P("lon", None, "lat"),
        P("lon", "lat", None),
    )
    return jax.shard_map(shards, mesh=mesh, in_specs=in_specs, out_specs=out_specs, check_vma=False)
```

```python
import functools

import jax
import jax.numpy as jnp
from jax import lax
from jax.experimental import pallas as pl
from jax.experimental.pallas import tpu as pltpu
from jax.sharding import PartitionSpec as P

D = 1024
NH = 32
WIN = 7
ROWS_DEV = 7
COLS_DEV = 21
PITCH = 24
TOK = ROWS_DEV * PITCH
EXPERTS = 64
CAP = 5
LANES = 128
BLOCKS = D // LANES
SLOTS = EXPERTS * CAP
SEND_ROWS = 2 * CAP * BLOCKS
BACK_ROWS = CAP * BLOCKS + 8
SHARE_ROWS = 40
PAY_ROWS = TOK + 8
WIDE = D + LANES

norm_eps = 1e-05
zloss_weight = 0.25
bf16 = jnp.bfloat16
f32 = jnp.float32
MEBI = 1024 * 1024


def call(kernel, vmem, out_shape, flops, moved, scratch=(), **kwargs):
    return pl.pallas_call(
        kernel,
        out_shape=out_shape,
        scratch_shapes=list(scratch),
        compiler_params=pltpu.CompilerParams(vmem_limit_bytes=vmem * MEBI),
        cost_estimate=pl.CostEstimate(flops=flops, bytes_accessed=moved, transcendentals=0),
        **kwargs,
    )


def mm(left, right):
    return lax.dot_general(left, right, (((1,), (0,)), ((), ())), preferred_element_type=f32)


def mm_cols(left, right):
    return lax.dot_general(left, right, (((1,), (1,)), ((), ())), preferred_element_type=f32)


def mm_rows(left, right):
    return lax.dot_general(left, right, (((0,), (0,)), ((), ())), preferred_element_type=f32)


def shape(dims, kind):
    return jax.ShapeDtypeStruct(dims, kind)


def iota(dims, axis):
    return lax.broadcasted_iota(jnp.int32, dims, axis)


def split3(value):
    high = value.astype(bf16)
    rest = value - high.astype(f32)
    middle = rest.astype(bf16)
    return (high, middle, (rest - middle.astype(f32)).astype(bf16))


def softmax_parts(logits):
    held = jnp.where(iota(logits.shape, 1) < EXPERTS, logits, -1e30)
    top = jnp.max(held, axis=-1, keepdims=True)
    raised = jnp.exp(held - top)
    total = jnp.sum(raised, axis=-1, keepdims=True)
    return (raised / total, top + jnp.log(total))


def three_logits(rows, split_router):
    triple = mm_cols(rows, split_router)
    return triple[:, 2 * LANES :] + triple[:, LANES : 2 * LANES] + triple[:, :LANES]


def front_kernel(
    resid_ref, grad_ref, gain_ref, router_ref, ids_ref, slots_ref,
    send_ref, split_ref, z_ref, normed_ref, stats_ref, back_ref, rows, folded, target_ref,
):
    target_ref[...] = jnp.full((2, 2 * TOK), -1, jnp.int32)
    back_ref[...] = jnp.full((2, TOK), -1, jnp.int32)
    for row in range(ROWS_DEV):
        ids = ids_ref[row]
        spots = slots_ref[row]
        base = row * PITCH
        back_ref[:, base : base + COLS_DEV] = spots * EXPERTS + ids
        target_ref[:, base : base + COLS_DEV] = ids * (2 * CAP) + spots
        target_ref[:, TOK + base : TOK + base + COLS_DEV] = ids * (2 * CAP) + spots + CAP
    rows[...] = jnp.zeros_like(rows)
    for row in range(ROWS_DEV):
        rows[row * PITCH : row * PITCH + COLS_DEV, :] = resid_ref[row].astype(f32)
        base = TOK + row * PITCH
        rows[base : base + COLS_DEV, :] = grad_ref[row].astype(f32)
    resid = rows[:TOK, :]
    center = resid - jnp.mean(resid, axis=-1, keepdims=True)
    inv_std = lax.rsqrt(jnp.mean(center * center, axis=-1, keepdims=True) + norm_eps)
    normed = center * inv_std
    normed_ref[...] = normed
    rows[:TOK, :] = normed * gain_ref[...]
    both = rows[...].astype(bf16)
    slot = iota((2 * SLOTS, 2 * TOK), 0)
    pick = jnp.where(
        (slot == target_ref[0:1, :]) | (slot == target_ref[1:2, :]), 1.0, 0.0
    ).astype(bf16)
    for pair in range(BLOCKS // 2):
        got = mm(pick, both[:, pair * 2 * LANES : (pair + 1) * 2 * LANES])
        for half in range(2):
            folded[pl.ds(2 * pair + half, 2 * SLOTS, stride=BLOCKS), :] = got[
                :, half * LANES : (half + 1) * LANES
            ]
    send_ref[...] = folded[...].astype(bf16)
    empty = jnp.zeros((LANES - EXPERTS, D), bf16)
    for index, part in enumerate(split3(router_ref[...])):
        split_ref[index * LANES : index * LANES + EXPERTS, :] = part
        split_ref[index * LANES + EXPERTS : (index + 1) * LANES, :] = empty
    z_ref[...] = jnp.where(iota((PAY_ROWS, 1), 0) < TOK, rows[:PAY_ROWS, :], 0.0).astype(bf16)
    probs, log_total = softmax_parts(three_logits(both[:PAY_ROWS, :], split_ref[...]))
    stats_ref[:, :LANES] = probs[:TOK]
    stats_ref[:, LANES : 2 * LANES] = jnp.broadcast_to(log_total[:TOK], (TOK, LANES))
    stats_ref[:, 2 * LANES :] = jnp.broadcast_to(inv_std, (TOK, LANES))


def front(resid, grad, gain, router_t, ids, slots):
    return call(
        front_kernel,
        56,
        (
            shape((EXPERTS * SEND_ROWS, LANES), bf16),
            shape((3 * LANES, D), bf16),
            shape((PAY_ROWS, D), bf16),
            shape((TOK, D), f32),
            shape((TOK, 3 * LANES), f32),
            shape((2, TOK), jnp.int32),
        ),
        4_600_000_000,
        4_000_000,
        [
            pltpu.VMEM((2 * TOK, D), f32),
            pltpu.VMEM((EXPERTS * SEND_ROWS, LANES), f32),
            pltpu.VMEM((2, 2 * TOK), jnp.int32),
        ],
    )(resid, grad, gain, router_t, ids, slots)


PARTS = (3 * EXPERTS, 2 * EXPERTS)


def unfold_kernel(got_ref, first_ref, second_ref, wide):
    wide[...] = got_ref[...].astype(f32)
    for c in range(2 * CAP):
        ref, place = (first_ref, c % CAP) if c % CAP < 3 else (second_ref, c % CAP - 3)
        base = place * EXPERTS + (c // CAP) * ref.shape[0] // 2
        for s in range(BLOCKS):
            ref[base : base + EXPERTS, s * LANES : (s + 1) * LANES] = wide[
                pl.ds(c * BLOCKS + s, EXPERTS, stride=SEND_ROWS), :
            ].astype(bf16)


def unfold(got):
    return call(
        unfold_kernel,
        14,
        tuple(shape((2 * part, D), bf16) for part in PARTS),
        3_900_000_000,
        2_600_000,
        [pltpu.VMEM((EXPERTS * SEND_ROWS, LANES), f32)],
    )(got)


FF_TILE = 256


def expert_kernel(count, expert_ref, *refs):
    chunks = refs[:count]
    in_ref, out_w_ref, split_ref, near_ref, far_ref, cu_ref, dh_ref = refs[count : count + 7]
    inputs, grads, total, dc, comb = refs[count + 7 :]
    step = pl.program_id(0)
    rows = inputs.shape[0]

    @pl.when(step == 0)
    def _():
        base = 0
        for ref in chunks:
            part = ref.shape[0] // 2
            inputs[base : base + part, :] = ref[:part, :]
            grads[base : base + part, :] = ref[part:, :]
            base += part
        probs, _unused = softmax_parts(three_logits(inputs[...], split_ref[...]))
        mine = jnp.where(iota(probs.shape, 1) == expert_ref[0], probs, 0.0)
        weight = jnp.sum(mine, axis=-1, keepdims=True).astype(bf16).astype(f32)
        comb[...] = jnp.broadcast_to(weight, (rows, LANES))
        dc[...] = jnp.zeros_like(dc)
        total[...] = jnp.zeros_like(total)

    weight_in = in_ref[...]
    hidden = mm(inputs[...], weight_in)
    grad_w = mm_cols(grads[...], out_w_ref[...])
    cdf = 0.5 * (1.0 + lax.erf(hidden * 0.7071067811865476))
    active = hidden * cdf
    slope = cdf + hidden * jnp.exp(-0.5 * hidden * hidden) * 0.3989422804014327
    dc[...] += jnp.broadcast_to(jnp.sum(active * grad_w, axis=-1, keepdims=True), (rows, LANES))
    weight = comb[:, 0:1]
    cu_ref[...] = (weight * active).astype(bf16)
    grad_hidden = (weight * grad_w * slope).astype(bf16)
    dh_ref[...] = grad_hidden
    total[...] += mm_cols(grad_hidden, weight_in)

    @pl.when(step == pl.num_programs(0) - 1)
    def _():
        for index, ref in enumerate((near_ref, far_ref)):
            span = slice(index * rows // 2, (index + 1) * rows // 2)
            ref[:, :D] = total[span, :].astype(bf16)
            ref[:, D:] = dc[span, :].astype(bf16)


def experts(expert, chunks, weight_in, weight_out, split_router):
    width = weight_in.shape[1]
    count = len(chunks)
    rows = sum(chunk.shape[0] for chunk in chunks) // 2
    whole = lambda dims: pl.BlockSpec(dims, lambda j: (0,) * len(dims))
    return call(
        functools.partial(expert_kernel, count),
        56 if count == 4 else 30,
        (
            shape((rows // 2, WIDE), bf16),
            shape((rows // 2, WIDE), bf16),
            shape((rows, width), bf16),
            shape((rows, width), bf16),
        ),
        22 * rows * D * width,
        12_000_000,
        [
            pltpu.VMEM((rows, D), bf16),
            pltpu.VMEM((rows, D), bf16),
            pltpu.VMEM((rows, D), f32),
            pltpu.VMEM((rows, LANES), f32),
            pltpu.VMEM((rows, LANES), f32),
        ],
        grid=(width // FF_TILE,),
        in_specs=[pl.BlockSpec(memory_space=pltpu.SMEM)]
        + [whole(chunk.shape) for chunk in chunks]
        + [
            pl.BlockSpec((D, FF_TILE), lambda j: (0, j)),
            pl.BlockSpec((FF_TILE, D), lambda j: (j, 0)),
            whole((3 * LANES, D)),
        ],
        out_specs=(
            whole((rows // 2, WIDE)),
            whole((rows // 2, WIDE)),
            pl.BlockSpec((rows, FF_TILE), lambda j: (0, j)),
            pl.BlockSpec((rows, FF_TILE), lambda j: (0, j)),
        ),
    )(expert, *chunks, weight_in, weight_out, split_router)


def weight_kernel(count, *refs):
    left, right, (out_ref, left_rows, right_rows) = (refs[:count], refs[count:-3], refs[-3:])

    def gather(parts, stack):
        base = 0
        for ref in parts:
            stack[base : base + ref.shape[0], :] = ref[...]
            base += ref.shape[0]

    @pl.when(pl.program_id(0) == 0)
    def _():
        gather(right, right_rows)

    gather(left, left_rows)
    out_ref[...] = mm_rows(left_rows[...], right_rows[...]).astype(bf16)


def weight_grad(left, right):
    block = 256

    def rows(pair):
        return pair[0].shape[0] // (1 if pair[1] is None else 2)

    def spec(pair, wide):
        half = pair[1] or 0
        if wide:
            return pl.BlockSpec((rows(pair), D), lambda j: (half, 0))
        return pl.BlockSpec((rows(pair), block), lambda j: (half, j))

    total = sum(rows(pair) for pair in left)
    return call(
        functools.partial(weight_kernel, len(left)),
        56,
        shape((D, D), bf16),
        1_000_000,
        1_000_000,
        [pltpu.VMEM((total, block), bf16), pltpu.VMEM((total, D), bf16)],
        grid=(D // block,),
        in_specs=[spec(pair, False) for pair in left] + [spec(pair, True) for pair in right],
        out_specs=pl.BlockSpec((block, D), lambda j: (j, 0)),
    )(*[pair[0] for pair in left], *[pair[0] for pair in right])


def fold_kernel(own_ref, near_ref, first_ref, second_ref, out_ref, folded, total):
    total[...] = own_ref[...].astype(f32) + near_ref[...].astype(f32)
    total[: PARTS[0], :] += first_ref[...].astype(f32)
    total[PARTS[0] :, :] += second_ref[...].astype(f32)
    for c in range(CAP):
        part = total[c * EXPERTS : (c + 1) * EXPERTS, :]
        for s in range(BLOCKS):
            folded[pl.ds(c * BLOCKS + s, EXPERTS, stride=BACK_ROWS), :] = part[
                :, s * LANES : (s + 1) * LANES
            ]
        folded[pl.ds(CAP * BLOCKS + c, EXPERTS, stride=BACK_ROWS), :] = part[:, D:]
    for spare in range(CAP * BLOCKS + CAP, BACK_ROWS):
        folded[pl.ds(spare, EXPERTS, stride=BACK_ROWS), :] = jnp.zeros((EXPERTS, LANES), f32)
    out_ref[...] = folded[...].astype(bf16)


def fold(own, near, first, second):
    return call(
        fold_kernel,
        14,
        shape((EXPERTS * BACK_ROWS, LANES), bf16),
        3_800_000_000,
        3_000_000,
        [pltpu.VMEM((EXPERTS * BACK_ROWS, LANES), f32), pltpu.VMEM((SLOTS, WIDE), f32)],
    )(own, near, first, second)


def middle_kernel(
    back_ref, target_ref, normed_ref, stats_ref, grad_ref, gain_ref, router_ref, proj_ref,
    resid_ref, attn_ref, pay_ref, wide, table, rows,
):
    wide[...] = back_ref[...].astype(f32)
    lane = iota((EXPERTS, LANES), 1)
    same = lane == iota((EXPERTS, LANES), 0)
    for c in range(CAP):
        span = slice(c * EXPERTS, (c + 1) * EXPERTS)
        for s in range(BLOCKS):
            table[span, s * LANES : (s + 1) * LANES] = wide[
                pl.ds(c * BLOCKS + s, EXPERTS, stride=BACK_ROWS), :
            ].astype(bf16)
        weights = wide[pl.ds(CAP * BLOCKS + c, EXPERTS, stride=BACK_ROWS), :]
        table[span, D:] = jnp.where(same, weights, 0.0).astype(bf16)
    slot = iota((SLOTS, TOK), 0)
    pick = jnp.where(
        (slot == target_ref[0:1, :]) | (slot == target_ref[1:2, :]), 1.0, 0.0
    ).astype(bf16)
    routed = mm_rows(pick, table[...])
    grad_probs = routed[:, D:]
    probs = stats_ref[:, :LANES]
    log_total = stats_ref[:, LANES : 2 * LANES]
    inv_std = stats_ref[:, 2 * LANES : 2 * LANES + 1]
    grad_logits = (
        probs * (grad_probs - jnp.sum(probs * grad_probs, axis=-1, keepdims=True))
        + 2.0 * zloss_weight * log_total * probs
    )
    grad_z = routed[:, :D] + jnp.dot(
        grad_logits[:, :EXPERTS], router_ref[...], precision=lax.Precision.HIGHEST,
        preferred_element_type=f32,
    )
    normed = normed_ref[...]
    gain_term = jnp.sum(grad_z * normed, axis=0, keepdims=True)
    rows[...] = jnp.zeros_like(rows)
    for row in range(ROWS_DEV):
        rows[row * PITCH : row * PITCH + COLS_DEV, :] = grad_ref[row].astype(f32)
    grad_normed = grad_z * gain_ref[...]
    rows[:TOK, :] = rows[:TOK, :] + inv_std * (
        grad_normed
        - jnp.mean(grad_normed, axis=-1, keepdims=True)
        - normed * jnp.mean(grad_normed * normed, axis=-1, keepdims=True)
    )
    for row in range(ROWS_DEV):
        resid_ref[row] = rows[row * PITCH : row * PITCH + COLS_DEV, :].astype(bf16)
    low = rows[...].astype(bf16)
    rows[...] = mm_cols(low, proj_ref[...])
    for row in range(ROWS_DEV):
        attn_ref[row] = rows[row * PITCH : row * PITCH + COLS_DEV, :].astype(bf16)
    high, middle, last = (part.astype(f32) for part in split3(gain_term))
    extra = iota((PAY_ROWS, 1), 0)
    rows[...] = jnp.where(
        extra < TOK,
        low.astype(f32),
        jnp.where(
            extra == TOK, high, jnp.where(extra == TOK + 1, middle, jnp.where(extra == TOK + 2, last, 0.0))
        ),
    )
    pay_ref[:, :D] = rows[...].astype(bf16)
    upper = grad_logits.astype(bf16).astype(f32)
    lower = (grad_logits - upper).astype(bf16).astype(f32)
    mixed = upper + pltpu.roll(lower, EXPERTS, 1)
    pay_ref[:, D:] = jnp.concatenate([mixed, jnp.zeros((PAY_ROWS - TOK, LANES), f32)], axis=0).astype(bf16)


def middle(back, targets, normed, stats, grad, gain, router_t, out_proj):
    return call(
        middle_kernel,
        56,
        (
            shape((ROWS_DEV, COLS_DEV, D), bf16),
            shape((ROWS_DEV, COLS_DEV, D), bf16),
            shape((PAY_ROWS, WIDE), bf16),
        ),
        7_000_000_000,
        6_000_000,
        [
            pltpu.VMEM((EXPERTS * BACK_ROWS, LANES), f32),
            pltpu.VMEM((SLOTS, WIDE), bf16),
            pltpu.VMEM((PAY_ROWS, D), f32),
        ],
    )(back, targets, normed, stats, grad, gain, router_t, out_proj)


SHARED = EXPERTS * SHARE_ROWS
QUARTER = D // 4


def share_kernel(core_ref, pay_ref, pay_near_ref, side_ref, side_near_ref, out_ref, folded):
    both = ((pay_ref, side_ref), (pay_near_ref, side_near_ref))
    gain = jnp.zeros((1, D), f32)
    at = iota((16, 1), 0)
    for pay, _unused in both:
        last = pay[PAY_ROWS - 16 :, :D].astype(f32)
        gain += jnp.sum(jnp.where((at >= 8) & (at < 11), last, 0.0), axis=0, keepdims=True)
    same = iota((QUARTER, QUARTER), 0) == iota((QUARTER, QUARTER), 1)
    lane = iota((QUARTER, LANES), 1)
    step = SHARE_ROWS // 4
    for block in range(2):
        z_at = slice(block * QUARTER, (block + 1) * QUARTER)
        a_at = slice((2 + block) * QUARTER, (3 + block) * QUARTER)
        proj = sum(mm_rows(side[:, a_at], pay[:, :D]) for pay, side in both)
        router = sum(mm_rows(side[:, z_at], pay[:, D:]) for pay, side in both)
        mine = jnp.zeros((1, QUARTER), f32)
        for core in range(2):
            place = (2 * block + core) * QUARTER
            mine += jnp.where(core_ref[0] == core, gain[:, place : place + QUARTER], 0.0)
        column = jnp.sum(jnp.where(same, mine, 0.0), axis=-1, keepdims=True)
        router = router + pltpu.roll(router, EXPERTS, 1)
        extra = jnp.where(lane < EXPERTS, router, jnp.where(lane == EXPERTS, column, 0.0))
        upper = extra.astype(bf16).astype(f32)
        base = block * SHARED
        for s in range(BLOCKS):
            folded[pl.ds(base + s, QUARTER, stride=step), :] = proj[:, s * LANES : (s + 1) * LANES]
        folded[pl.ds(base + BLOCKS, QUARTER, stride=step), :] = upper
        folded[pl.ds(base + BLOCKS + 1, QUARTER, stride=step), :] = extra - upper
    out_ref[...] = folded[...].astype(bf16)


def share(core, *arrays):
    inner = pl.BlockSpec(memory_space=pltpu.VMEM)
    return call(
        share_kernel,
        20,
        shape((2 * SHARED, LANES), bf16),
        3_900_000_000,
        4_000_000,
        [pltpu.VMEM((2 * SHARED, LANES), f32)],
        in_specs=[pl.BlockSpec(memory_space=pltpu.SMEM)] + [inner] * 4,
    )(core, *arrays)


def tally_kernel(got_ref, out_ref):
    out_ref[...] = sum(got_ref[k].astype(f32) for k in range(got_ref.shape[0]))


def tally(got):
    return call(tally_kernel, 8, shape(got.shape[1:], f32), 1_000_000_000, 1_500_000)(got)


def finish_kernel(got_ref, proj_ref, router_ref, gain_ref):
    total = sum(got_ref[k] for k in range(got_ref.shape[0]))
    step = SHARE_ROWS // 4
    lane = iota((1, 4), 1)
    gain = jnp.zeros((1, 4), f32)
    for r in range(4):
        for s in range(BLOCKS):
            proj_ref[r : r + 1, s * LANES : (s + 1) * LANES] = total[r * step + s : r * step + s + 1]
        at = r * step + BLOCKS
        extra = total[at : at + 1] + total[at + 1 : at + 2]
        router_ref[r : r + 1, :] = extra[:, :EXPERTS]
        gain = jnp.where(lane == r, extra[:, EXPERTS : EXPERTS + 1], gain)
    gain_ref[...] = gain


def finish(got):
    return call(
        finish_kernel,
        4,
        (shape((4, D), f32), shape((4, EXPERTS), f32), shape((1, 4), f32)),
        1_000_000_000,
        200_000,
    )(got)


def swap(value, step):
    return lax.ppermute(value, "lat", [(k, k ^ step) for k in range(4)])


def exchange(value, axes="lon", groups=None):
    return lax.all_to_all(
        value, axes, split_axis=0, concat_axis=0, tiled=True, axis_index_groups=groups
    )


def spread(value):
    return exchange(value.reshape(EXPERTS, -1, LANES)).reshape(-1, LANES)


RING = 8
ALONG = [[line * RING + k for k in range(RING)] for line in range(EXPERTS // RING)]
ACROSS = [
    [
        (2 * row + core) * EXPERTS + line * RING + k
        for row in range(2)
        for line in range(EXPERTS // RING)
    ]
    for core in range(2)
    for k in range(RING)
]


KEYS = 64
GROUPS = D // LANES
PER = LANES // (D // NH)
SPAN = 40
LINES = 32


def head_masks(kind):
    lane = iota((KEYS, LANES), 1) // (D // NH)
    return [jnp.where(lane == j, 1.0, 0.0).astype(kind) for j in range(PER)]


def by_head(values, masks):
    return jnp.concatenate([values * mask for mask in masks], axis=0)


def halves(values, pick):
    first = iota(values.shape, 1) < KEYS
    left = pick(values, first)
    right = pick(values, jnp.logical_not(first))
    return jnp.where(first, left, right)


def half_sum(values):
    return halves(
        values, lambda v, m: jnp.sum(jnp.where(m, v, 0.0), axis=-1, keepdims=True)
    )


def half_max(values):
    return halves(
        values, lambda v, m: jnp.max(jnp.where(m, v, -3e38), axis=-1, keepdims=True)
    )


def attend_kernel(outer, shift_ref, own_ref, *refs):
    shifted = shift_ref[0]
    if outer:
        left_ref, right_ref, done_ref, q_ref, k_ref, v_ref, p_ref, att_ref, wide, win, back, flat = refs
        windows = (0, 3)
    else:
        q_ref, k_ref, v_ref, p_ref, out_ref, wide, win = refs
        windows = (1, 2)
    factor = (D // NH) ** (-0.5)
    for row in range(ROWS_DEV):
        for i in range(3):
            line = row * 3 + i
            wide[line, COLS_DEV + 2 * WIN - 3 : SPAN, :] = jnp.zeros((8, D), f32)
            wide[line, WIN : WIN + COLS_DEV, :] = own_ref[row, i].astype(f32)
            if outer:
                wide[line, :WIN, :] = left_ref[row, i].astype(f32)
                wide[line, WIN + COLS_DEV : 2 * WIN + COLS_DEV, :] = right_ref[row, i].astype(f32)
            else:
                wide[line, :WIN, :] = jnp.zeros((WIN, D), f32)
                wide[line, WIN + COLS_DEV : 2 * WIN + COLS_DEV, :] = jnp.zeros((WIN, D), f32)
            wide[line] = pltpu.roll(wide[line], SPAN - WIN + shifted, 0)
            for at_w, w in enumerate(windows):
                win[i, at_w, row * 8 : (row + 1) * 8, :] = wide[line, WIN * w : WIN * w + 8, :]
    win[:, :, KEYS - 8 :, :] = jnp.zeros((3, 2, 8, D), f32)
    masks = head_masks(bf16)
    key = iota((KEYS, LANES), 1) & (KEYS - 1)
    real = (key < ROWS_DEV * 8) & ((key & 7) < WIN)

    def window(w, carry):
        q_ref[w] = win[0, w].astype(bf16)
        k_ref[w] = win[1, w].astype(bf16)
        v_ref[w] = win[2, w].astype(bf16)
        for block in range(GROUPS):
            at = slice(block * LANES, (block + 1) * LANES)
            keys = by_head(k_ref[w, :, at], masks)
            values = by_head(v_ref[w, :, at], masks)
            scores = mm_cols(q_ref[w, :, at], keys) * factor
            parts = []
            for half in range(2):
                held = jnp.where(real, scores[:, half * LANES : (half + 1) * LANES], -1e30)
                raised = jnp.exp(held - half_max(held))
                probs = raised / half_sum(raised)
                base = (2 * block + half) * LANES
                p_ref[w, :, base : base + LANES] = probs
                parts.append(probs.astype(bf16))
            win[0, w, :, at] = mm(jnp.concatenate(parts, axis=1), values)
        return carry

    lax.fori_loop(0, 2, window, 0)
    if not outer:
        out_ref[...] = win[0].astype(bf16)
        return
    win[1] = done_ref[...].astype(f32)
    flat[...] = jnp.zeros_like(flat)
    for row in range(ROWS_DEV):
        span = slice(row * 8, (row + 1) * 8)
        back[row, 0:8, :] = win[0, 0, span, :]
        back[row, WIN : WIN + 8, :] = win[1, 0, span, :]
        back[row, 2 * WIN : 2 * WIN + 8, :] = win[1, 1, span, :]
        back[row, 3 * WIN : 3 * WIN + 8, :] = win[0, 1, span, :]
        turned = pltpu.roll(back[row], jnp.where(shifted == 0, 0, LINES - shifted), 0)
        flat[row * PITCH : row * PITCH + COLS_DEV, :] = turned[:COLS_DEV]
    att_ref[...] = flat[...].astype(bf16)


def attend(shifted, own, edges=()):
    inner = pl.BlockSpec(memory_space=pltpu.VMEM)
    last = shape((2, KEYS, D), bf16)
    scratch = [pltpu.VMEM((3 * ROWS_DEV, SPAN, D), f32), pltpu.VMEM((3, 2, KEYS, D), f32)]
    if edges:
        last = shape((PAY_ROWS, D), bf16)
        scratch += [pltpu.VMEM((ROWS_DEV, LINES, D), f32), pltpu.VMEM((PAY_ROWS, D), f32)]
    return call(
        functools.partial(attend_kernel, bool(edges)),
        56,
        (*3 * [shape((2, KEYS, D), bf16)], shape((2, KEYS, 2 * D), f32), last),
        1_000_000 if edges else 9_000_000_000,
        1_000_000 if edges else 6_000_000,
        scratch,
        in_specs=[pl.BlockSpec(memory_space=pltpu.SMEM)] + [inner] * (1 + len(edges)),
    )(shifted, own, *edges)


def attend_grad_kernel(
    outer, shift_ref, own_ref, q_ref, k_ref, v_ref, p_ref, *refs
):
    shifted = shift_ref[0]
    if outer:
        left_ref, right_ref, done_ref, out_ref, wide, win, back = refs
        win[:, 1:3] = done_ref[...].astype(f32)
        windows = (0, 3)
    else:
        out_ref, wide, win = refs
        windows = (1, 2)
    factor = (D // NH) ** (-0.5)
    valid = jnp.where(iota((8, 1), 0) < WIN, 1.0, 0.0)
    for row in range(ROWS_DEV):
        wide[row, COLS_DEV + 2 * WIN - 3 : SPAN, :] = jnp.zeros((8, D), f32)
        wide[row, WIN : WIN + COLS_DEV, :] = own_ref[row].astype(f32)
        if outer:
            wide[row, :WIN, :] = left_ref[row].astype(f32)
            wide[row, WIN + COLS_DEV : 2 * WIN + COLS_DEV, :] = right_ref[row].astype(f32)
        else:
            wide[row, :WIN, :] = jnp.zeros((WIN, D), f32)
            wide[row, WIN + COLS_DEV : 2 * WIN + COLS_DEV, :] = jnp.zeros((WIN, D), f32)
        wide[row] = pltpu.roll(wide[row], SPAN - WIN + shifted, 0)
        for w in windows:
            win[0, w, row * 8 : (row + 1) * 8, :] = wide[row, WIN * w : WIN * w + 8, :] * valid
    for w in windows:
        win[0, w, KEYS - 8 :, :] = jnp.zeros((8, D), f32)
    masks = head_masks(bf16)
    wide_masks = head_masks(f32)

    def gathered(values):
        return sum(
            wide_masks[j] * values[j * KEYS : (j + 1) * KEYS] for j in range(PER)
        )

    def window(at_w, carry):
        w = 3 * at_w if outer else at_w + 1
        for block in range(GROUPS):
            at = slice(block * LANES, (block + 1) * LANES)
            upstream = win[0, w, :, at].astype(bf16)
            keys = by_head(k_ref[at_w, :, at], masks)
            values = by_head(v_ref[at_w, :, at], masks)
            grad_probs = mm_cols(upstream, values)
            low = []
            grads = []
            for half in range(2):
                base = (2 * block + half) * LANES
                probs = p_ref[at_w, :, base : base + LANES]
                part = grad_probs[:, half * LANES : (half + 1) * LANES]
                grads.append((probs * (part - half_sum(part * probs)) * factor).astype(bf16))
                low.append(probs.astype(bf16))
            grad_scores = jnp.concatenate(grads, axis=1)
            win[0, w, :, at] = mm(grad_scores, keys)
            win[1, w, :, at] = gathered(mm_rows(grad_scores, q_ref[at_w, :, at]))
            win[2, w, :, at] = gathered(mm_rows(jnp.concatenate(low, axis=1), upstream))
        return carry

    lax.fori_loop(0, 2, window, 0)
    if not outer:
        out_ref[...] = win[:, 1:3].astype(bf16)
        return
    for row in range(ROWS_DEV):
        for i in range(3):
            line = row * 3 + i
            for w in range(4):
                back[line, WIN * w : WIN * w + 8, :] = win[i, w, row * 8 : (row + 1) * 8, :]
            turned = pltpu.roll(back[line], jnp.where(shifted == 0, 0, LINES - shifted), 0)
            out_ref[row, i] = turned[:COLS_DEV].astype(bf16)


def attend_grad(shifted, own, saved, edges=()):
    inner = pl.BlockSpec(memory_space=pltpu.VMEM)
    part = shape((3, 2, KEYS, D), bf16)
    scratch = [pltpu.VMEM((ROWS_DEV, SPAN, D), f32), pltpu.VMEM((3, 4, KEYS, D), f32)]
    if edges:
        part = shape((ROWS_DEV, 3, COLS_DEV, D), bf16)
        scratch.append(pltpu.VMEM((3 * ROWS_DEV, LINES, D), f32))
    return call(
        functools.partial(attend_grad_kernel, bool(edges)),
        56,
        part,
        10_000_000_000,
        6_000_000,
        scratch,
        in_specs=[pl.BlockSpec(memory_space=pltpu.SMEM)] + [inner] * (5 + len(edges)),
    )(shifted, own, *saved, *edges)


def halo(values, axis):
    count = lax.axis_size("lon")
    length = values.shape[axis]
    left = lax.ppermute(
        lax.slice_in_dim(values, length - WIN, length, axis=axis),
        "lon",
        [(i, (i + 1) % count) for i in range(count)],
    )
    right = lax.ppermute(
        lax.slice_in_dim(values, 0, WIN, axis=axis),
        "lon",
        [((i + 1) % count, i) for i in range(count)],
    )
    return (left, values, right)


def shards(
    resid, qkv, out_proj, norm_gain, router, w_in, w_out, expert_ids, slots, shifts, grad_out
):
    lat = lax.axis_index("lat")
    lon = lax.axis_index("lon")
    router_t = router.T
    gain = norm_gain.reshape(1, D)
    places = (expert_ids.transpose(0, 2, 1), slots.transpose(0, 2, 1))
    send, split_router, routed_in, normed, stats, back_at = front(
        resid, grad_out, gain, router_t, *places
    )
    shifted = shifts[lat].reshape(1)
    send, here = lax.optimization_barrier((send, qkv.transpose(0, 2, 1, 3)))
    got = spread(send)
    *inside, attended = attend(shifted, here)
    got, attended, here = lax.optimization_barrier((got, attended, here))
    own = unfold(got)
    far = [swap(part, 2) for part in own]
    near = [swap(part, 1) for part in own]

    expert = lon.astype(jnp.int32).reshape(1)
    weights = (w_in[0], w_out[0], split_router)
    chunks = [*own, *near]
    dx_own, dx_near, cu, dh = experts(expert, chunks, *weights)
    cus, dhs, far_sums = ([cu], [dh], [])
    far[0], dx_own = lax.optimization_barrier((far[0], dx_own))
    near_sum = swap(dx_near, 1)
    for part in range(2):
        pair = [far[part], swap(far[part], 1)]
        if part == 1:
            *pair, pair_sum = lax.optimization_barrier((*pair, pair_sum))
            far_sums.append(swap(pair_sum, 2))
        dx_far, dx_cross, cu, dh = experts(expert, pair, *weights)
        if part == 0:
            far[1], dx_far, dx_cross = lax.optimization_barrier((far[1], dx_far, dx_cross))
            dx_cross = swap(dx_cross, 1)
        else:
            dx_cross, far_sums[0] = lax.optimization_barrier((swap(dx_cross, 1), far_sums[0]))
        pair_sum = (dx_far.astype(f32) + dx_cross.astype(f32)).astype(bf16)
        chunks += pair
        cus.append(cu)
        dhs.append(dh)
    pair_sum, here = lax.optimization_barrier((pair_sum, here))
    left, here, right = halo(here, 2)
    far_sums.append(swap(pair_sum, 2))
    folded = fold(dx_own, near_sum, *far_sums)
    folded, chunks, cus, dhs, left, right = lax.optimization_barrier(
        (folded, chunks, cus, dhs, left, right)
    )
    back = spread(folded)
    *outside, attended = attend(shifted, here, (left, right, attended))
    core = lat & 1

    def side_for(core):
        return jnp.concatenate(
            [
                lax.dynamic_slice_in_dim(values, (2 * block + core) * QUARTER, QUARTER, 1)
                for values in (routed_in, attended)
                for block in range(2)
            ],
            axis=1,
        )

    sides = (side_for(core), side_for(1 - core))
    d_w_in = weight_grad([(chunk, 0) for chunk in chunks], [(dh, None) for dh in dhs])
    back, sides, d_w_in = lax.optimization_barrier((back, sides, d_w_in))
    d_resid, d_attn, pay = middle(
        back, back_at, normed, stats, grad_out, gain, router_t, out_proj
    )
    pays = (pay, swap(pay, 1))
    shares = share(core.astype(jnp.int32).reshape(1), *pays, sides[0], swap(sides[1], 1))
    shares, d_attn, chunks, cus = lax.optimization_barrier((shares, d_attn, chunks, cus))
    d_w_out = weight_grad([(cu, None) for cu in cus], [(chunk, 1) for chunk in chunks])
    left, d_attn, right = halo(d_attn, 1)
    middle_grads = attend_grad(shifted, d_attn, inside)
    shares = shares.reshape(2 * RING, RING * SHARE_ROWS, LANES)
    shares = exchange(shares, ("lat", "lon"), ACROSS)
    shares, middle_grads, d_w_out = lax.optimization_barrier((shares, middle_grads, d_w_out))
    shares = tally(shares).reshape(RING, SHARE_ROWS, LANES)
    left, right, shares = lax.optimization_barrier((left, right, shares))
    d_qkv = attend_grad(shifted, d_attn, outside, (left, right, middle_grads)).transpose(0, 2, 1, 3)
    proj_share, router_share, gain_share = finish(exchange(shares, groups=ALONG))
    return (
        d_resid,
        d_qkv,
        proj_share,
        gain_share.reshape(4),
        router_share,
        d_w_in[None],
        d_w_out[None],
    )


def solution(mesh):
    in_specs = (
        P("lat", "lon", None),
        P("lat", "lon", None, None),
        P(),
        P(),
        P(),
        P("lon", None, "lat"),
        P("lon", "lat", None),
        P("lat", "lon", None),
        P("lat", "lon", None),
        P(),
        P("lat", "lon", None),
    )
    out_specs = (
        P("lat", "lon", None),
        P("lat", "lon", None, None),
        P(("lat", "lon"), None),
        P(("lat", "lon")),
        P(("lat", "lon"), None),
        P("lon", None, "lat"),
        P("lon", "lat", None),
    )
    return jax.shard_map(shards, mesh=mesh, in_specs=in_specs, out_specs=out_specs, check_vma=False)
```

```python
import functools

import jax
import jax.numpy as jnp
from jax import lax
from jax.experimental import pallas as pl
from jax.experimental.pallas import tpu as pltpu
from jax.sharding import PartitionSpec as P

D = 1024
NH = 32
WIN = 7
ROWS_DEV = 7
COLS_DEV = 21
PITCH = 24
TOK = ROWS_DEV * PITCH
EXPERTS = 64
CAP = 5
LANES = 128
BLOCKS = D // LANES
SLOTS = EXPERTS * CAP
SEND_ROWS = 2 * CAP * BLOCKS
BACK_ROWS = CAP * BLOCKS + 8
SHARE_ROWS = 40
PAY_ROWS = TOK + 8
WIDE = D + LANES

norm_eps = 1e-05
zloss_weight = 0.25
bf16 = jnp.bfloat16
f32 = jnp.float32
MEBI = 1024 * 1024


def call(kernel, vmem, out_shape, flops, moved, scratch=(), **kwargs):
    return pl.pallas_call(
        kernel,
        out_shape=out_shape,
        scratch_shapes=list(scratch),
        compiler_params=pltpu.CompilerParams(vmem_limit_bytes=vmem * MEBI),
        cost_estimate=pl.CostEstimate(flops=flops, bytes_accessed=moved, transcendentals=0),
        **kwargs,
    )


def mm(left, right):
    return lax.dot_general(left, right, (((1,), (0,)), ((), ())), preferred_element_type=f32)


def mm_cols(left, right):
    return lax.dot_general(left, right, (((1,), (1,)), ((), ())), preferred_element_type=f32)


def mm_rows(left, right):
    return lax.dot_general(left, right, (((0,), (0,)), ((), ())), preferred_element_type=f32)


def shape(dims, kind):
    return jax.ShapeDtypeStruct(dims, kind)


def iota(dims, axis):
    return lax.broadcasted_iota(jnp.int32, dims, axis)


def split3(value):
    high = value.astype(bf16)
    rest = value - high.astype(f32)
    middle = rest.astype(bf16)
    return (high, middle, (rest - middle.astype(f32)).astype(bf16))


def softmax_parts(logits):
    held = jnp.where(iota(logits.shape, 1) < EXPERTS, logits, -1e30)
    top = jnp.max(held, axis=-1, keepdims=True)
    raised = jnp.exp(held - top)
    total = jnp.sum(raised, axis=-1, keepdims=True)
    return (raised / total, top + jnp.log(total))


def three_logits(rows, split_router):
    triple = mm_cols(rows, split_router)
    return triple[:, 2 * LANES :] + triple[:, LANES : 2 * LANES] + triple[:, :LANES]


def front_kernel(
    resid_ref, grad_ref, gain_ref, router_ref, ids_ref, slots_ref,
    send_ref, split_ref, z_ref, normed_ref, stats_ref, back_ref, rows, folded, target_ref,
):
    target_ref[...] = jnp.full((2, 2 * TOK), -1, jnp.int32)
    back_ref[...] = jnp.full((2, TOK), -1, jnp.int32)
    for row in range(ROWS_DEV):
        ids = ids_ref[row]
        spots = slots_ref[row]
        base = row * PITCH
        back_ref[:, base : base + COLS_DEV] = spots * EXPERTS + ids
        target_ref[:, base : base + COLS_DEV] = ids * (2 * CAP) + spots
        target_ref[:, TOK + base : TOK + base + COLS_DEV] = ids * (2 * CAP) + spots + CAP
    rows[...] = jnp.zeros_like(rows)
    for row in range(ROWS_DEV):
        rows[row * PITCH : row * PITCH + COLS_DEV, :] = resid_ref[row].astype(f32)
        base = TOK + row * PITCH
        rows[base : base + COLS_DEV, :] = grad_ref[row].astype(f32)
    resid = rows[:TOK, :]
    center = resid - jnp.mean(resid, axis=-1, keepdims=True)
    inv_std = lax.rsqrt(jnp.mean(center * center, axis=-1, keepdims=True) + norm_eps)
    normed = center * inv_std
    normed_ref[...] = normed
    rows[:TOK, :] = normed * gain_ref[...]
    both = rows[...].astype(bf16)
    slot = iota((2 * SLOTS, 2 * TOK), 0)
    pick = jnp.where(
        (slot == target_ref[0:1, :]) | (slot == target_ref[1:2, :]), 1.0, 0.0
    ).astype(bf16)
    for pair in range(BLOCKS // 2):
        got = mm(pick, both[:, pair * 2 * LANES : (pair + 1) * 2 * LANES])
        for half in range(2):
            folded[pl.ds(2 * pair + half, 2 * SLOTS, stride=BLOCKS), :] = got[
                :, half * LANES : (half + 1) * LANES
            ]
    send_ref[...] = folded[...].astype(bf16)
    empty = jnp.zeros((LANES - EXPERTS, D), bf16)
    for index, part in enumerate(split3(router_ref[...])):
        split_ref[index * LANES : index * LANES + EXPERTS, :] = part
        split_ref[index * LANES + EXPERTS : (index + 1) * LANES, :] = empty
    z_ref[...] = jnp.where(iota((PAY_ROWS, 1), 0) < TOK, rows[:PAY_ROWS, :], 0.0).astype(bf16)
    probs, log_total = softmax_parts(three_logits(both[:PAY_ROWS, :], split_ref[...]))
    stats_ref[:, :LANES] = probs[:TOK]
    stats_ref[:, LANES : 2 * LANES] = jnp.broadcast_to(log_total[:TOK], (TOK, LANES))
    stats_ref[:, 2 * LANES :] = jnp.broadcast_to(inv_std, (TOK, LANES))


def front(resid, grad, gain, router_t, ids, slots):
    return call(
        front_kernel,
        56,
        (
            shape((EXPERTS * SEND_ROWS, LANES), bf16),
            shape((3 * LANES, D), bf16),
            shape((PAY_ROWS, D), bf16),
            shape((TOK, D), f32),
            shape((TOK, 3 * LANES), f32),
            shape((2, TOK), jnp.int32),
        ),
        4_600_000_000,
        4_000_000,
        [
            pltpu.VMEM((2 * TOK, D), f32),
            pltpu.VMEM((EXPERTS * SEND_ROWS, LANES), f32),
            pltpu.VMEM((2, 2 * TOK), jnp.int32),
        ],
    )(resid, grad, gain, router_t, ids, slots)


PARTS = (3 * EXPERTS, 2 * EXPERTS)


def unfold_kernel(got_ref, first_ref, second_ref, wide):
    wide[...] = got_ref[...].astype(f32)
    for c in range(2 * CAP):
        ref, place = (first_ref, c % CAP) if c % CAP < 3 else (second_ref, c % CAP - 3)
        base = place * EXPERTS + (c // CAP) * ref.shape[0] // 2
        for s in range(BLOCKS):
            ref[base : base + EXPERTS, s * LANES : (s + 1) * LANES] = wide[
                pl.ds(c * BLOCKS + s, EXPERTS, stride=SEND_ROWS), :
            ].astype(bf16)


def unfold(got):
    return call(
        unfold_kernel,
        14,
        tuple(shape((2 * part, D), bf16) for part in PARTS),
        3_900_000_000,
        2_600_000,
        [pltpu.VMEM((EXPERTS * SEND_ROWS, LANES), f32)],
    )(got)


FF_TILE = 256


def expert_kernel(count, expert_ref, *refs):
    chunks = refs[:count]
    in_ref, out_w_ref, split_ref, near_ref, far_ref, cu_ref, dh_ref = refs[count : count + 7]
    inputs, grads, total, dc, comb = refs[count + 7 :]
    step = pl.program_id(0)
    rows = inputs.shape[0]

    @pl.when(step == 0)
    def _():
        base = 0
        for ref in chunks:
            part = ref.shape[0] // 2
            inputs[base : base + part, :] = ref[:part, :]
            grads[base : base + part, :] = ref[part:, :]
            base += part
        probs, _unused = softmax_parts(three_logits(inputs[...], split_ref[...]))
        mine = jnp.where(iota(probs.shape, 1) == expert_ref[0], probs, 0.0)
        weight = jnp.sum(mine, axis=-1, keepdims=True).astype(bf16).astype(f32)
        comb[...] = jnp.broadcast_to(weight, (rows, LANES))
        dc[...] = jnp.zeros_like(dc)
        total[...] = jnp.zeros_like(total)

    weight_in = in_ref[...]
    hidden = mm(inputs[...], weight_in)
    grad_w = mm_cols(grads[...], out_w_ref[...])
    cdf = 0.5 * (1.0 + lax.erf(hidden * 0.7071067811865476))
    active = hidden * cdf
    slope = cdf + hidden * jnp.exp(-0.5 * hidden * hidden) * 0.3989422804014327
    dc[...] += jnp.broadcast_to(jnp.sum(active * grad_w, axis=-1, keepdims=True), (rows, LANES))
    weight = comb[:, 0:1]
    cu_ref[...] = (weight * active).astype(bf16)
    grad_hidden = (weight * grad_w * slope).astype(bf16)
    dh_ref[...] = grad_hidden
    total[...] += mm_cols(grad_hidden, weight_in)

    @pl.when(step == pl.num_programs(0) - 1)
    def _():
        for index, ref in enumerate((near_ref, far_ref)):
            span = slice(index * rows // 2, (index + 1) * rows // 2)
            ref[:, :D] = total[span, :].astype(bf16)
            ref[:, D:] = dc[span, :].astype(bf16)


def experts(expert, chunks, weight_in, weight_out, split_router):
    width = weight_in.shape[1]
    count = len(chunks)
    rows = sum(chunk.shape[0] for chunk in chunks) // 2
    whole = lambda dims: pl.BlockSpec(dims, lambda j: (0,) * len(dims))
    return call(
        functools.partial(expert_kernel, count),
        56 if count == 4 else 30,
        (
            shape((rows // 2, WIDE), bf16),
            shape((rows // 2, WIDE), bf16),
            shape((rows, width), bf16),
            shape((rows, width), bf16),
        ),
        22 * rows * D * width,
        12_000_000,
        [
            pltpu.VMEM((rows, D), bf16),
            pltpu.VMEM((rows, D), bf16),
            pltpu.VMEM((rows, D), f32),
            pltpu.VMEM((rows, LANES), f32),
            pltpu.VMEM((rows, LANES), f32),
        ],
        grid=(width // FF_TILE,),
        in_specs=[pl.BlockSpec(memory_space=pltpu.SMEM)]
        + [whole(chunk.shape) for chunk in chunks]
        + [
            pl.BlockSpec((D, FF_TILE), lambda j: (0, j)),
            pl.BlockSpec((FF_TILE, D), lambda j: (j, 0)),
            whole((3 * LANES, D)),
        ],
        out_specs=(
            whole((rows // 2, WIDE)),
            whole((rows // 2, WIDE)),
            pl.BlockSpec((rows, FF_TILE), lambda j: (0, j)),
            pl.BlockSpec((rows, FF_TILE), lambda j: (0, j)),
        ),
    )(expert, *chunks, weight_in, weight_out, split_router)


def weight_kernel(count, *refs):
    left, right, (out_ref, left_rows, right_rows) = (refs[:count], refs[count:-3], refs[-3:])

    def gather(parts, stack):
        base = 0
        for ref in parts:
            stack[base : base + ref.shape[0], :] = ref[...]
            base += ref.shape[0]

    @pl.when(pl.program_id(0) == 0)
    def _():
        gather(right, right_rows)

    gather(left, left_rows)
    out_ref[...] = mm_rows(left_rows[...], right_rows[...]).astype(bf16)


def weight_grad(left, right):
    block = 256

    def rows(pair):
        return pair[0].shape[0] // (1 if pair[1] is None else 2)

    def spec(pair, wide):
        half = pair[1] or 0
        if wide:
            return pl.BlockSpec((rows(pair), D), lambda j: (half, 0))
        return pl.BlockSpec((rows(pair), block), lambda j: (half, j))

    total = sum(rows(pair) for pair in left)
    return call(
        functools.partial(weight_kernel, len(left)),
        56,
        shape((D, D), bf16),
        1_000_000,
        1_000_000,
        [pltpu.VMEM((total, block), bf16), pltpu.VMEM((total, D), bf16)],
        grid=(D // block,),
        in_specs=[spec(pair, False) for pair in left] + [spec(pair, True) for pair in right],
        out_specs=pl.BlockSpec((block, D), lambda j: (j, 0)),
    )(*[pair[0] for pair in left], *[pair[0] for pair in right])


def fold_kernel(own_ref, near_ref, first_ref, second_ref, out_ref, folded, total):
    total[...] = own_ref[...].astype(f32) + near_ref[...].astype(f32)
    total[: PARTS[0], :] += first_ref[...].astype(f32)
    total[PARTS[0] :, :] += second_ref[...].astype(f32)
    for c in range(CAP):
        part = total[c * EXPERTS : (c + 1) * EXPERTS, :]
        for s in range(BLOCKS):
            folded[pl.ds(c * BLOCKS + s, EXPERTS, stride=BACK_ROWS), :] = part[
                :, s * LANES : (s + 1) * LANES
            ]
        folded[pl.ds(CAP * BLOCKS + c, EXPERTS, stride=BACK_ROWS), :] = part[:, D:]
    for spare in range(CAP * BLOCKS + CAP, BACK_ROWS):
        folded[pl.ds(spare, EXPERTS, stride=BACK_ROWS), :] = jnp.zeros((EXPERTS, LANES), f32)
    out_ref[...] = folded[...].astype(bf16)


def fold(own, near, first, second):
    return call(
        fold_kernel,
        14,
        shape((EXPERTS * BACK_ROWS, LANES), bf16),
        3_800_000_000,
        3_000_000,
        [pltpu.VMEM((EXPERTS * BACK_ROWS, LANES), f32), pltpu.VMEM((SLOTS, WIDE), f32)],
    )(own, near, first, second)


def middle_kernel(
    back_ref, target_ref, normed_ref, stats_ref, grad_ref, gain_ref, router_ref, proj_ref,
    resid_ref, attn_ref, pay_ref, wide, table, rows,
):
    wide[...] = back_ref[...].astype(f32)
    lane = iota((EXPERTS, LANES), 1)
    same = lane == iota((EXPERTS, LANES), 0)
    for c in range(CAP):
        span = slice(c * EXPERTS, (c + 1) * EXPERTS)
        for s in range(BLOCKS):
            table[span, s * LANES : (s + 1) * LANES] = wide[
                pl.ds(c * BLOCKS + s, EXPERTS, stride=BACK_ROWS), :
            ].astype(bf16)
        weights = wide[pl.ds(CAP * BLOCKS + c, EXPERTS, stride=BACK_ROWS), :]
        table[span, D:] = jnp.where(same, weights, 0.0).astype(bf16)
    slot = iota((SLOTS, TOK), 0)
    pick = jnp.where(
        (slot == target_ref[0:1, :]) | (slot == target_ref[1:2, :]), 1.0, 0.0
    ).astype(bf16)
    routed = mm_rows(pick, table[...])
    grad_probs = routed[:, D:]
    probs = stats_ref[:, :LANES]
    log_total = stats_ref[:, LANES : 2 * LANES]
    inv_std = stats_ref[:, 2 * LANES : 2 * LANES + 1]
    grad_logits = (
        probs * (grad_probs - jnp.sum(probs * grad_probs, axis=-1, keepdims=True))
        + 2.0 * zloss_weight * log_total * probs
    )
    grad_z = routed[:, :D] + jnp.dot(
        grad_logits[:, :EXPERTS], router_ref[...], precision=lax.Precision.HIGHEST,
        preferred_element_type=f32,
    )
    normed = normed_ref[...]
    gain_term = jnp.sum(grad_z * normed, axis=0, keepdims=True)
    rows[...] = jnp.zeros_like(rows)
    for row in range(ROWS_DEV):
        rows[row * PITCH : row * PITCH + COLS_DEV, :] = grad_ref[row].astype(f32)
    grad_normed = grad_z * gain_ref[...]
    rows[:TOK, :] = rows[:TOK, :] + inv_std * (
        grad_normed
        - jnp.mean(grad_normed, axis=-1, keepdims=True)
        - normed * jnp.mean(grad_normed * normed, axis=-1, keepdims=True)
    )
    for row in range(ROWS_DEV):
        resid_ref[row] = rows[row * PITCH : row * PITCH + COLS_DEV, :].astype(bf16)
    low = rows[...].astype(bf16)
    rows[...] = mm_cols(low, proj_ref[...])
    for row in range(ROWS_DEV):
        attn_ref[row] = rows[row * PITCH : row * PITCH + COLS_DEV, :].astype(bf16)
    high, middle, last = (part.astype(f32) for part in split3(gain_term))
    extra = iota((PAY_ROWS, 1), 0)
    rows[...] = jnp.where(
        extra < TOK,
        low.astype(f32),
        jnp.where(
            extra == TOK, high, jnp.where(extra == TOK + 1, middle, jnp.where(extra == TOK + 2, last, 0.0))
        ),
    )
    pay_ref[:, :D] = rows[...].astype(bf16)
    upper = grad_logits.astype(bf16).astype(f32)
    lower = (grad_logits - upper).astype(bf16).astype(f32)
    mixed = upper + pltpu.roll(lower, EXPERTS, 1)
    pay_ref[:, D:] = jnp.concatenate([mixed, jnp.zeros((PAY_ROWS - TOK, LANES), f32)], axis=0).astype(bf16)


def middle(back, targets, normed, stats, grad, gain, router_t, out_proj):
    return call(
        middle_kernel,
        56,
        (
            shape((ROWS_DEV, COLS_DEV, D), bf16),
            shape((ROWS_DEV, COLS_DEV, D), bf16),
            shape((PAY_ROWS, WIDE), bf16),
        ),
        7_000_000_000,
        6_000_000,
        [
            pltpu.VMEM((EXPERTS * BACK_ROWS, LANES), f32),
            pltpu.VMEM((SLOTS, WIDE), bf16),
            pltpu.VMEM((PAY_ROWS, D), f32),
        ],
    )(back, targets, normed, stats, grad, gain, router_t, out_proj)


SHARED = EXPERTS * SHARE_ROWS
QUARTER = D // 4


def share_kernel(core_ref, pay_ref, pay_near_ref, side_ref, side_near_ref, out_ref, folded):
    both = ((pay_ref, side_ref), (pay_near_ref, side_near_ref))
    gain = jnp.zeros((1, D), f32)
    at = iota((16, 1), 0)
    for pay, _unused in both:
        last = pay[PAY_ROWS - 16 :, :D].astype(f32)
        gain += jnp.sum(jnp.where((at >= 8) & (at < 11), last, 0.0), axis=0, keepdims=True)
    same = iota((QUARTER, QUARTER), 0) == iota((QUARTER, QUARTER), 1)
    lane = iota((QUARTER, LANES), 1)
    step = SHARE_ROWS // 4
    for block in range(2):
        z_at = slice(block * QUARTER, (block + 1) * QUARTER)
        a_at = slice((2 + block) * QUARTER, (3 + block) * QUARTER)
        proj = sum(mm_rows(side[:, a_at], pay[:, :D]) for pay, side in both)
        router = sum(mm_rows(side[:, z_at], pay[:, D:]) for pay, side in both)
        mine = jnp.zeros((1, QUARTER), f32)
        for core in range(2):
            place = (2 * block + core) * QUARTER
            mine += jnp.where(core_ref[0] == core, gain[:, place : place + QUARTER], 0.0)
        column = jnp.sum(jnp.where(same, mine, 0.0), axis=-1, keepdims=True)
        router = router + pltpu.roll(router, EXPERTS, 1)
        extra = jnp.where(lane < EXPERTS, router, jnp.where(lane == EXPERTS, column, 0.0))
        upper = extra.astype(bf16).astype(f32)
        base = block * SHARED
        for s in range(BLOCKS):
            folded[pl.ds(base + s, QUARTER, stride=step), :] = proj[:, s * LANES : (s + 1) * LANES]
        folded[pl.ds(base + BLOCKS, QUARTER, stride=step), :] = upper
        folded[pl.ds(base + BLOCKS + 1, QUARTER, stride=step), :] = extra - upper
    out_ref[...] = folded[...].astype(bf16)


def share(core, *arrays):
    inner = pl.BlockSpec(memory_space=pltpu.VMEM)
    return call(
        share_kernel,
        20,
        shape((2 * SHARED, LANES), bf16),
        3_900_000_000,
        4_000_000,
        [pltpu.VMEM((2 * SHARED, LANES), f32)],
        in_specs=[pl.BlockSpec(memory_space=pltpu.SMEM)] + [inner] * 4,
    )(core, *arrays)


def tally_kernel(got_ref, out_ref):
    out_ref[...] = sum(got_ref[k].astype(f32) for k in range(got_ref.shape[0]))


def tally(got):
    return call(tally_kernel, 8, shape(got.shape[1:], f32), 1_000_000_000, 1_500_000)(got)


def finish_kernel(got_ref, proj_ref, router_ref, gain_ref):
    total = sum(got_ref[k] for k in range(got_ref.shape[0]))
    step = SHARE_ROWS // 4
    lane = iota((1, 4), 1)
    gain = jnp.zeros((1, 4), f32)
    for r in range(4):
        for s in range(BLOCKS):
            proj_ref[r : r + 1, s * LANES : (s + 1) * LANES] = total[r * step + s : r * step + s + 1]
        at = r * step + BLOCKS
        extra = total[at : at + 1] + total[at + 1 : at + 2]
        router_ref[r : r + 1, :] = extra[:, :EXPERTS]
        gain = jnp.where(lane == r, extra[:, EXPERTS : EXPERTS + 1], gain)
    gain_ref[...] = gain


def finish(got):
    return call(
        finish_kernel,
        4,
        (shape((4, D), f32), shape((4, EXPERTS), f32), shape((1, 4), f32)),
        1_000_000_000,
        200_000,
    )(got)


def swap(value, step):
    return lax.ppermute(value, "lat", [(k, k ^ step) for k in range(4)])


def exchange(value, axes="lon", groups=None):
    return lax.all_to_all(
        value, axes, split_axis=0, concat_axis=0, tiled=True, axis_index_groups=groups
    )


def spread(value):
    return exchange(value.reshape(EXPERTS, -1, LANES)).reshape(-1, LANES)


RING = 8
ALONG = [[line * RING + k for k in range(RING)] for line in range(EXPERTS // RING)]
ACROSS = [
    [
        (2 * row + core) * EXPERTS + line * RING + k
        for row in range(2)
        for line in range(EXPERTS // RING)
    ]
    for core in range(2)
    for k in range(RING)
]


KEYS = 64
GROUPS = D // LANES
PER = LANES // (D // NH)
SPAN = 40
LINES = 32


def head_masks(kind):
    lane = iota((KEYS, LANES), 1) // (D // NH)
    return [jnp.where(lane == j, 1.0, 0.0).astype(kind) for j in range(PER)]


def by_head(values, masks):
    return jnp.concatenate([values * mask for mask in masks], axis=0)


def halves(values, pick):
    first = iota(values.shape, 1) < KEYS
    left = pick(values, first)
    right = pick(values, jnp.logical_not(first))
    return jnp.where(first, left, right)


def half_sum(values):
    return halves(
        values, lambda v, m: jnp.sum(jnp.where(m, v, 0.0), axis=-1, keepdims=True)
    )


def half_max(values):
    return halves(
        values, lambda v, m: jnp.max(jnp.where(m, v, -3e38), axis=-1, keepdims=True)
    )


def attend_kernel(outer, shift_ref, own_ref, *refs):
    shifted = shift_ref[0]
    if outer:
        left_ref, right_ref, done_ref, q_ref, k_ref, v_ref, p_ref, att_ref, wide, win, back, flat = refs
        windows = (0, 3)
    else:
        q_ref, k_ref, v_ref, p_ref, out_ref, wide, win = refs
        windows = (1, 2)
    factor = (D // NH) ** (-0.5)
    for row in range(ROWS_DEV):
        for i in range(3):
            line = row * 3 + i
            wide[line, COLS_DEV + 2 * WIN - 3 : SPAN, :] = jnp.zeros((8, D), f32)
            wide[line, WIN : WIN + COLS_DEV, :] = own_ref[row, i].astype(f32)
            if outer:
                wide[line, :WIN, :] = left_ref[row, i].astype(f32)
                wide[line, WIN + COLS_DEV : 2 * WIN + COLS_DEV, :] = right_ref[row, i].astype(f32)
            else:
                wide[line, :WIN, :] = jnp.zeros((WIN, D), f32)
                wide[line, WIN + COLS_DEV : 2 * WIN + COLS_DEV, :] = jnp.zeros((WIN, D), f32)
            wide[line] = pltpu.roll(wide[line], SPAN - WIN + shifted, 0)
            for at_w, w in enumerate(windows):
                win[i, at_w, row * 8 : (row + 1) * 8, :] = wide[line, WIN * w : WIN * w + 8, :]
    win[:, :, KEYS - 8 :, :] = jnp.zeros((3, 2, 8, D), f32)
    masks = head_masks(bf16)
    key = iota((KEYS, LANES), 1) & (KEYS - 1)
    real = (key < ROWS_DEV * 8) & ((key & 7) < WIN)

    def window(w, carry):
        q_ref[w] = win[0, w].astype(bf16)
        k_ref[w] = win[1, w].astype(bf16)
        v_ref[w] = win[2, w].astype(bf16)
        for block in range(GROUPS):
            at = slice(block * LANES, (block + 1) * LANES)
            keys = by_head(k_ref[w, :, at], masks)
            values = by_head(v_ref[w, :, at], masks)
            scores = mm_cols(q_ref[w, :, at], keys) * factor
            parts = []
            for half in range(2):
                held = jnp.where(real, scores[:, half * LANES : (half + 1) * LANES], -1e30)
                raised = jnp.exp(held - half_max(held))
                probs = raised / half_sum(raised)
                base = (2 * block + half) * LANES
                p_ref[w, :, base : base + LANES] = probs
                parts.append(probs.astype(bf16))
            win[0, w, :, at] = mm(jnp.concatenate(parts, axis=1), values)
        return carry

    lax.fori_loop(0, 2, window, 0)
    if not outer:
        out_ref[...] = win[0].astype(bf16)
        return
    win[1] = done_ref[...].astype(f32)
    flat[...] = jnp.zeros_like(flat)
    for row in range(ROWS_DEV):
        span = slice(row * 8, (row + 1) * 8)
        back[row, 0:8, :] = win[0, 0, span, :]
        back[row, WIN : WIN + 8, :] = win[1, 0, span, :]
        back[row, 2 * WIN : 2 * WIN + 8, :] = win[1, 1, span, :]
        back[row, 3 * WIN : 3 * WIN + 8, :] = win[0, 1, span, :]
        turned = pltpu.roll(back[row], jnp.where(shifted == 0, 0, LINES - shifted), 0)
        flat[row * PITCH : row * PITCH + COLS_DEV, :] = turned[:COLS_DEV]
    att_ref[...] = flat[...].astype(bf16)


def attend(shifted, own, edges=()):
    inner = pl.BlockSpec(memory_space=pltpu.VMEM)
    last = shape((2, KEYS, D), bf16)
    scratch = [pltpu.VMEM((3 * ROWS_DEV, SPAN, D), f32), pltpu.VMEM((3, 2, KEYS, D), f32)]
    if edges:
        last = shape((PAY_ROWS, D), bf16)
        scratch += [pltpu.VMEM((ROWS_DEV, LINES, D), f32), pltpu.VMEM((PAY_ROWS, D), f32)]
    return call(
        functools.partial(attend_kernel, bool(edges)),
        56,
        (*3 * [shape((2, KEYS, D), bf16)], shape((2, KEYS, 2 * D), f32), last),
        1_000_000 if edges else 9_000_000_000,
        1_000_000 if edges else 6_000_000,
        scratch,
        in_specs=[pl.BlockSpec(memory_space=pltpu.SMEM)] + [inner] * (1 + len(edges)),
    )(shifted, own, *edges)


def attend_grad_kernel(
    outer, shift_ref, own_ref, q_ref, k_ref, v_ref, p_ref, *refs
):
    shifted = shift_ref[0]
    if outer:
        left_ref, right_ref, done_ref, out_ref, wide, win, back = refs
        win[:, 1:3] = done_ref[...].astype(f32)
        windows = (0, 3)
    else:
        out_ref, wide, win = refs
        windows = (1, 2)
    factor = (D // NH) ** (-0.5)
    valid = jnp.where(iota((8, 1), 0) < WIN, 1.0, 0.0)
    for row in range(ROWS_DEV):
        wide[row, COLS_DEV + 2 * WIN - 3 : SPAN, :] = jnp.zeros((8, D), f32)
        wide[row, WIN : WIN + COLS_DEV, :] = own_ref[row].astype(f32)
        if outer:
            wide[row, :WIN, :] = left_ref[row].astype(f32)
            wide[row, WIN + COLS_DEV : 2 * WIN + COLS_DEV, :] = right_ref[row].astype(f32)
        else:
            wide[row, :WIN, :] = jnp.zeros((WIN, D), f32)
            wide[row, WIN + COLS_DEV : 2 * WIN + COLS_DEV, :] = jnp.zeros((WIN, D), f32)
        wide[row] = pltpu.roll(wide[row], SPAN - WIN + shifted, 0)
        for w in windows:
            win[0, w, row * 8 : (row + 1) * 8, :] = wide[row, WIN * w : WIN * w + 8, :] * valid
    for w in windows:
        win[0, w, KEYS - 8 :, :] = jnp.zeros((8, D), f32)
    masks = head_masks(bf16)
    wide_masks = head_masks(f32)

    def gathered(values):
        return sum(
            wide_masks[j] * values[j * KEYS : (j + 1) * KEYS] for j in range(PER)
        )

    def window(at_w, carry):
        w = 3 * at_w if outer else at_w + 1
        for block in range(GROUPS):
            at = slice(block * LANES, (block + 1) * LANES)
            upstream = win[0, w, :, at].astype(bf16)
            keys = by_head(k_ref[at_w, :, at], masks)
            values = by_head(v_ref[at_w, :, at], masks)
            grad_probs = mm_cols(upstream, values)
            low = []
            grads = []
            for half in range(2):
                base = (2 * block + half) * LANES
                probs = p_ref[at_w, :, base : base + LANES]
                part = grad_probs[:, half * LANES : (half + 1) * LANES]
                grads.append((probs * (part - half_sum(part * probs)) * factor).astype(bf16))
                low.append(probs.astype(bf16))
            grad_scores = jnp.concatenate(grads, axis=1)
            win[0, w, :, at] = mm(grad_scores, keys)
            win[1, w, :, at] = gathered(mm_rows(grad_scores, q_ref[at_w, :, at]))
            win[2, w, :, at] = gathered(mm_rows(jnp.concatenate(low, axis=1), upstream))
        return carry

    lax.fori_loop(0, 2, window, 0)
    if not outer:
        out_ref[...] = win[:, 1:3].astype(bf16)
        return
    for row in range(ROWS_DEV):
        for i in range(3):
            line = row * 3 + i
            for w in range(4):
                back[line, WIN * w : WIN * w + 8, :] = win[i, w, row * 8 : (row + 1) * 8, :]
            turned = pltpu.roll(back[line], jnp.where(shifted == 0, 0, LINES - shifted), 0)
            out_ref[row, i] = turned[:COLS_DEV].astype(bf16)


def attend_grad(shifted, own, saved, edges=()):
    inner = pl.BlockSpec(memory_space=pltpu.VMEM)
    part = shape((3, 2, KEYS, D), bf16)
    scratch = [pltpu.VMEM((ROWS_DEV, SPAN, D), f32), pltpu.VMEM((3, 4, KEYS, D), f32)]
    if edges:
        part = shape((ROWS_DEV, 3, COLS_DEV, D), bf16)
        scratch.append(pltpu.VMEM((3 * ROWS_DEV, LINES, D), f32))
    return call(
        functools.partial(attend_grad_kernel, bool(edges)),
        56,
        part,
        10_000_000_000,
        6_000_000,
        scratch,
        in_specs=[pl.BlockSpec(memory_space=pltpu.SMEM)] + [inner] * (5 + len(edges)),
    )(shifted, own, *saved, *edges)


def halo(values, axis):
    count = lax.axis_size("lon")
    length = values.shape[axis]
    left = lax.ppermute(
        lax.slice_in_dim(values, length - WIN, length, axis=axis),
        "lon",
        [(i, (i + 1) % count) for i in range(count)],
    )
    right = lax.ppermute(
        lax.slice_in_dim(values, 0, WIN, axis=axis),
        "lon",
        [((i + 1) % count, i) for i in range(count)],
    )
    return (left, values, right)


def shards(
    resid, qkv, out_proj, norm_gain, router, w_in, w_out, expert_ids, slots, shifts, grad_out
):
    lat = lax.axis_index("lat")
    lon = lax.axis_index("lon")
    router_t = router.T
    gain = norm_gain.reshape(1, D)
    places = (expert_ids.transpose(0, 2, 1), slots.transpose(0, 2, 1))
    send, split_router, routed_in, normed, stats, back_at = front(
        resid, grad_out, gain, router_t, *places
    )
    shifted = shifts[lat].reshape(1)
    send, here = lax.optimization_barrier((send, qkv.transpose(0, 2, 1, 3)))
    got = spread(send)
    *inside, attended = attend(shifted, here)
    got, attended, here = lax.optimization_barrier((got, attended, here))
    own = unfold(got)
    far = [swap(part, 2) for part in own]
    near = [swap(part, 1) for part in own]

    expert = lon.astype(jnp.int32).reshape(1)
    weights = (w_in[0], w_out[0], split_router)
    chunks = [*own, *near]
    dx_own, dx_near, cu, dh = experts(expert, chunks, *weights)
    cus, dhs, far_sums = ([cu], [dh], [])
    far[0], dx_own = lax.optimization_barrier((far[0], dx_own))
    near_sum = swap(dx_near, 1)
    for part in range(2):
        pair = [far[part], swap(far[part], 1)]
        if part == 1:
            *pair, pair_sum = lax.optimization_barrier((*pair, pair_sum))
            far_sums.append(swap(pair_sum, 2))
        dx_far, dx_cross, cu, dh = experts(expert, pair, *weights)
        if part == 0:
            far[1], dx_far, dx_cross = lax.optimization_barrier((far[1], dx_far, dx_cross))
            dx_cross = swap(dx_cross, 1)
        else:
            dx_cross, here = lax.optimization_barrier((dx_cross, here))
            left, here, right = halo(here, 2)
            dx_cross, far_sums[0] = lax.optimization_barrier((swap(dx_cross, 1), far_sums[0]))
        pair_sum = (dx_far.astype(f32) + dx_cross.astype(f32)).astype(bf16)
        chunks += pair
        cus.append(cu)
        dhs.append(dh)
    far_sums.append(swap(pair_sum, 2))
    near_sum, left, right = lax.optimization_barrier((near_sum, left, right))
    folded = fold(dx_own, near_sum, *far_sums)
    folded, chunks, cus, dhs, left, right = lax.optimization_barrier(
        (folded, chunks, cus, dhs, left, right)
    )
    back = spread(folded)
    *outside, attended = attend(shifted, here, (left, right, attended))
    core = lat & 1

    def side_for(core):
        return jnp.concatenate(
            [
                lax.dynamic_slice_in_dim(values, (2 * block + core) * QUARTER, QUARTER, 1)
                for values in (routed_in, attended)
                for block in range(2)
            ],
            axis=1,
        )

    sides = (side_for(core), side_for(1 - core))
    d_w_in = weight_grad([(chunk, 0) for chunk in chunks], [(dh, None) for dh in dhs])
    back, sides, d_w_in = lax.optimization_barrier((back, sides, d_w_in))
    d_resid, d_attn, pay = middle(
        back, back_at, normed, stats, grad_out, gain, router_t, out_proj
    )
    pays = (pay, swap(pay, 1))
    shares = share(core.astype(jnp.int32).reshape(1), *pays, sides[0], swap(sides[1], 1))
    shares, d_attn, chunks, cus = lax.optimization_barrier((shares, d_attn, chunks, cus))
    d_w_out = weight_grad([(cu, None) for cu in cus], [(chunk, 1) for chunk in chunks])
    left, d_attn, right = halo(d_attn, 1)
    middle_grads = attend_grad(shifted, d_attn, inside)
    shares = shares.reshape(2 * RING, RING * SHARE_ROWS, LANES)
    shares = exchange(shares, ("lat", "lon"), ACROSS)
    shares, middle_grads, d_w_out = lax.optimization_barrier((shares, middle_grads, d_w_out))
    shares = tally(shares).reshape(RING, SHARE_ROWS, LANES)
    left, right, shares = lax.optimization_barrier((left, right, shares))
    d_qkv = attend_grad(shifted, d_attn, outside, (left, right, middle_grads)).transpose(0, 2, 1, 3)
    proj_share, router_share, gain_share = finish(exchange(shares, groups=ALONG))
    return (
        d_resid,
        d_qkv,
        proj_share,
        gain_share.reshape(4),
        router_share,
        d_w_in[None],
        d_w_out[None],
    )


def solution(mesh):
    in_specs = (
        P("lat", "lon", None),
        P("lat", "lon", None, None),
        P(),
        P(),
        P(),
        P("lon", None, "lat"),
        P("lon", "lat", None),
        P("lat", "lon", None),
        P("lat", "lon", None),
        P(),
        P("lat", "lon", None),
    )
    out_specs = (
        P("lat", "lon", None),
        P("lat", "lon", None, None),
        P(("lat", "lon"), None),
        P(("lat", "lon")),
        P(("lat", "lon"), None),
        P("lon", None, "lat"),
        P("lon", "lat", None),
    )
    return jax.shard_map(shards, mesh=mesh, in_specs=in_specs, out_specs=out_specs, check_vma=False)
```
